32 devices in a mesh: grp: 4 (over x, core), wide: 8 (over z, y).
Axes of the slice: x: 2, y: 2, z: 4, core: 2. Of those that a mesh axis runs over, the one named last changes fastest.
Arguments:
- amplitudes: float32 [1024, 64, 512], P(('grp', 'wide')), may hold values from -6 to 6
- integrals: float32 [4, 512, 512], P('grp'), may hold values from -0.25 to 0.25
- base_residual: float32 [32, 64, 512], P(('grp', 'wide')), may hold values from -6 to 6
- occ_gap: float32 [32, 64], P(('grp', 'wide')), may hold values from 0.5 to 4
- virt_sum: float32 [512], replicated, may hold values from 0.5 to 4
- task_amp: int32 [32, 96], P(('grp', 'wide')), may hold values from 0 to 255, as said below
- task_int: int32 [32, 96], P(('grp', 'wide')), may hold values from 0 to 3
- task_res: int32 [32, 96], P(('grp', 'wide')), may hold values from 0 to 7, as said below
- task_count: int32 [32], P(('grp', 'wide')), may hold values from 12 to 96, as said below
- res_owner: int32 [4, 8], P('grp'), may hold values from 0 to 7, as said below
- amp_label: int32 [1024], P(('grp', 'wide')), may hold values from 0 to 3
- int_label: int32 [4], replicated, may hold values from 0 to 3
Outputs:
- doubles_residual: float32 [32, 64, 512], P(('grp', 'wide'))
The draws below stay inside these ranges and needn't reach their ends.
Inputs may be any that keep to these rules, and one draw needn't show every extreme that they name: `task_amp`: amplitude block t of a grp row is kept by the device of wide index t // 32 of that row, at its local position t % 32. Among the used slots of one device at most 12 name blocks kept by one device. `task_res`: among the used slots of one device at most 12 name tiles whose position (see res_owner) lies on one device. Slots from task_count on are unused; their entries are arbitrary values within the stated ranges. `res_owner`: each row is a permutation; position p of a grp row lies on the device of wide index p, at its local position p % 1.
All inputs are finite; a program needn't handle non-finite values.
Results may differ from the reference program's by a relative error of at most 0.0001.
Values sent between devices are 32-bit elements; how exact they have to be, the bound alone decides.
No kernel may reach another device: no remote copies, remote signals or barrier semaphores. Data moves between devices by JAX's collectives and lax.ppermute only.
A program may use at most 128 MiB of HBM per device.

```python
import jax
import jax.numpy as jnp
from jax import lax

TILE_ROWS = 64
BLOCK_COLS = 512
WINDOW = 512
TASK_SLOTS = 96
AMP_DEV = 32
RES_DEV = 1
INT_DEV = 1
AMP_ALL = 1024
RES_ALL = 32
INT_BLOCKS = 4
N_GRP = 4
N_WIDE = 8
DEVICES = 32


def spread_holders(counts, usable, slot_index, subkey):
    ends = jnp.cumsum(counts, axis=2)
    sorted_holder = jnp.sum((slot_index[None, None, :, None] >= ends[:, :, None, :]).astype(jnp.int32), axis=3)
    sorted_holder = jnp.minimum(sorted_holder, N_WIDE - 1).astype(jnp.int32)
    scores = jax.random.randint(subkey, usable.shape, 0, 1 << 20) * TASK_SLOTS + slot_index[None, None, :]
    scores = jnp.where(usable, scores, (1 << 20) * TASK_SLOTS + slot_index[None, None, :])
    order_of = jnp.argsort(scores, axis=2)
    return jnp.take_along_axis(sorted_holder, order_of, axis=2)


def layout(key):
    keys = jax.random.split(jax.random.fold_in(key, 101), 9)
    bucket = TASK_SLOTS // N_WIDE
    lane_ids = jnp.arange(N_WIDE, dtype=jnp.int32)
    busy_lane = jax.random.randint(keys[0], (N_GRP,), 0, N_WIDE)
    light_lane = (busy_lane + 1 + jax.random.randint(keys[8], (N_GRP,), 0, N_WIDE - 1)) % N_WIDE
    counts = jax.random.randint(keys[1], (N_GRP, N_WIDE, N_WIDE), 0, bucket + 1)
    full_mask = (lane_ids[None, None, :] == busy_lane[:, None, None]) | (lane_ids[None, :, None] == busy_lane[:, None, None])
    counts = jnp.where(full_mask, bucket, counts).astype(jnp.int32)
    light_mask = (lane_ids[None, :, None] == light_lane[:, None, None]) & (lane_ids[None, None, :] != busy_lane[:, None, None])
    counts = jnp.where(light_mask, 0, counts).astype(jnp.int32)
    owner_shuffle = jax.vmap(lambda subkey: jax.random.permutation(subkey, N_WIDE))(jax.random.split(keys[2], N_GRP))
    inverse = jnp.argsort(owner_shuffle, axis=1)
    res_counts = jnp.take_along_axis(counts, jnp.broadcast_to(inverse[:, None, :], counts.shape), axis=2)
    totals = jnp.sum(counts, axis=2).astype(jnp.int32)
    slot_index = jnp.arange(TASK_SLOTS, dtype=jnp.int32)
    usable = slot_index[None, None, :] < totals[:, :, None]
    amp_holder = spread_holders(counts, usable, slot_index, keys[3])
    res_holder = spread_holders(res_counts, usable, slot_index, keys[4])
    amp_slot = jax.random.randint(keys[5], usable.shape, 0, AMP_DEV)
    res_slot = jax.random.randint(keys[6], usable.shape, 0, RES_DEV)
    task_amp = amp_holder * AMP_DEV + amp_slot
    position = res_holder * RES_DEV + res_slot
    kept = jax.vmap(lambda subkey: jax.random.permutation(subkey, RES_DEV * N_WIDE))(jax.random.split(keys[7], N_GRP))
    kept_wide = jnp.broadcast_to(kept[:, None, :], (N_GRP, N_WIDE, RES_DEV * N_WIDE))
    task_res = jnp.take_along_axis(kept_wide, position, axis=2)
    return (task_amp.reshape(N_GRP * N_WIDE, TASK_SLOTS).astype(jnp.int32), task_res.reshape(N_GRP * N_WIDE, TASK_SLOTS).astype(jnp.int32), totals.reshape(N_GRP * N_WIDE).astype(jnp.int32), kept.astype(jnp.int32))


def draw_task_amp(key, part):
    return layout(key)[0]


def draw_task_res(key, part):
    return layout(key)[1]


def draw_task_count(key, part):
    return layout(key)[2]


def draw_res_owner(key, part):
    return layout(key)[3]


def touch_ends(values, key, least, largest):
    place = [jax.random.randint(jax.random.fold_in(key, axis), (), 0, length) for axis, length in enumerate(values.shape)]
    longest = values.shape.index(max(values.shape))
    beside = place[:longest] + [(place[longest] + 1) % values.shape[longest]] + place[longest + 1:]
    return values.at[tuple(place)].set(least).at[tuple(beside)].set(largest)


def block_levels(stream_key, extent, cuts, low, largest):
    def one(axis_at, shards_of):
        draws = jax.random.uniform(jax.random.fold_in(jax.random.fold_in(stream_key, 6), axis_at), (shards_of,), jnp.float32, low / len(cuts), largest / len(cuts))
        return jnp.repeat(jnp.exp(draws), extent[axis_at] // shards_of).reshape((-1,) + (1,) * (len(extent) - axis_at - 1))

    gain = one(*cuts[0])
    for cut in cuts[1:]:
        gain = gain * one(*cut)
    return gain


def noise(own_key, extent, deviation, most, shards=(), held_as=jnp.bfloat16):
    loudness = block_levels(own_key, extent, shards, -0.22, 0.18) if shards else 1.0
    values = jax.random.normal(own_key, extent, jnp.float32) * deviation * loudness
    return jnp.minimum(jnp.maximum(values, -most), most).astype(held_as)


def setup_inputs(seed: int = 0) -> dict:
    key_list = jax.random.split(jax.random.key(seed), 13)
    amplitudes = noise(key_list[0], (AMP_ALL, TILE_ROWS, BLOCK_COLS), 1.0, 6.0, ((0, 32),), jnp.float32)
    integrals = noise(key_list[1], (INT_BLOCKS, BLOCK_COLS, WINDOW), BLOCK_COLS ** -0.5, 0.25, ((0, 4),), jnp.float32)
    base_residual = noise(key_list[2], (RES_ALL, TILE_ROWS, WINDOW), 1.0, 6.0, ((0, 32),), jnp.float32)
    occ_gap = jnp.clip(0.5 + 3.5 * jax.random.uniform(key_list[3], (RES_ALL, TILE_ROWS), jnp.float32) ** block_levels(key_list[3], (RES_ALL, TILE_ROWS), ((0, 32),), -0.2, 0.2), 0.5, 4.0)
    virt_sum = jnp.clip(jax.random.uniform(key_list[4], (WINDOW,), jnp.float32, 0.5, 4.0), 0.5, 4.0)
    task_amp = draw_task_amp(jax.random.fold_in(key_list[12], 71), 0)
    task_int = touch_ends(jax.random.randint(key_list[6], (DEVICES, TASK_SLOTS), 0, INT_BLOCKS), jax.random.fold_in(key_list[6], 1), 0, INT_BLOCKS - 1).astype(jnp.int32)
    task_res = draw_task_res(jax.random.fold_in(key_list[12], 71), 0)
    task_count = draw_task_count(jax.random.fold_in(key_list[12], 71), 0)
    res_owner = draw_res_owner(jax.random.fold_in(key_list[12], 71), 0)
    amp_label = touch_ends(jax.random.randint(key_list[10], (AMP_ALL,), 0, 4), jax.random.fold_in(key_list[10], 1), 0, 3).astype(jnp.int32)
    int_label = touch_ends(jax.random.randint(key_list[11], (INT_BLOCKS,), 0, 4), jax.random.fold_in(key_list[11], 1), 0, 3).astype(jnp.int32)
    return dict(amplitudes=amplitudes, integrals=integrals, base_residual=base_residual, occ_gap=occ_gap, virt_sum=virt_sum, task_amp=task_amp, task_int=task_int, task_res=task_res, task_count=task_count, res_owner=res_owner, amp_label=amp_label, int_label=int_label)


def reference(amplitudes, integrals, base_residual, occ_gap, virt_sum, task_amp, task_int, task_res, task_count, res_owner, amp_label, int_label):
    row_tiles = AMP_DEV * N_WIDE
    row_res = RES_DEV * N_WIDE
    blocks = INT_DEV * N_GRP
    slot_index = jnp.arange(TASK_SLOTS, dtype=jnp.int32)
    pieces = []
    for row_group in range(N_GRP):
        lanes_of = slice(row_group * N_WIDE, (row_group + 1) * N_WIDE)
        usable = (slot_index[None, :] < task_count[lanes_of][:, None]).reshape(-1)
        amp_ids = (task_amp[lanes_of].reshape(-1) + row_group * row_tiles).astype(jnp.int32)
        int_ids = task_int[lanes_of].reshape(-1).astype(jnp.int32)
        parity = (amp_label[amp_ids] + int_label[int_ids]) % 2
        signs = jnp.where(usable, 1.0 - 2.0 * parity.astype(jnp.float32), 0.0).astype(jnp.float32)
        where_kept = jnp.argsort(res_owner[row_group]).astype(jnp.int32)
        position = where_kept[task_res[lanes_of].reshape(-1)].astype(jnp.int32)
        segment = (position * blocks + int_ids).astype(jnp.int32)
        phased = amplitudes[amp_ids] * signs[:, None, None]
        stacked = jax.ops.segment_sum(phased, segment, num_segments=row_res * blocks)
        stacked = stacked.reshape(row_res, blocks, TILE_ROWS, BLOCK_COLS)
        summed_all = jnp.einsum("pcik,ckl->pil", stacked, integrals, precision=lax.Precision.HIGHEST)
        rows_of = slice(row_group * row_res, (row_group + 1) * row_res)
        divisor = occ_gap[rows_of][:, :, None] + virt_sum[None, None, :]
        pieces.append((base_residual[rows_of] + summed_all) / divisor)
    return jnp.concatenate(pieces, axis=0)
```

```python
import functools

import jax
import jax.numpy as jnp
from jax import lax
from jax.experimental import pallas as pl
from jax.experimental.pallas import tpu as pltpu
from jax.sharding import PartitionSpec as P

LANES = 128


def split(x):
    hi = x.astype(jnp.bfloat16)
    return hi, (x - hi.astype(jnp.float32)).astype(jnp.bfloat16)


def swap(x, axis, k):
    n = lax.axis_size(axis)
    return lax.ppermute(x, axis, [(i, i ^ k) for i in range(n)])


def coefficients(lists_ref, amp_label_ref, owner_ref, int_label_ref, amp_dev, lanes, blocks):
    lane = lax.axis_index("wide")
    grp = lax.axis_index("grp")
    amp, cint, res, count = (lists_ref[i] for i in range(4))
    slot = lax.broadcasted_iota(jnp.int32, amp.shape, 1)
    local = amp - lane * amp_dev
    valid = (slot < count) & (local >= 0) & (local < amp_dev)
    pos = jnp.zeros_like(res)
    for p in range(lanes):
        pos = jnp.where(res == owner_ref[0, p], p, pos)
    seg = (pos ^ lane) * blocks + (cint ^ grp)
    seg = jnp.where(valid, seg, -1)
    rows = lanes * blocks
    row_id = lax.broadcasted_iota(jnp.int32, (rows, amp.shape[1]), 0)
    col_id = lax.broadcasted_iota(jnp.int32, (LANES, amp.shape[1]), 0)
    counts = jnp.zeros((rows, LANES), jnp.float32)
    for src in range(lanes):
        hit_row = jnp.where(row_id == seg[src : src + 1, :], 1.0, 0.0)
        hit_col = jnp.where(col_id == local[src : src + 1, :], 1.0, 0.0)
        counts += lax.dot_general(
            hit_row.astype(jnp.bfloat16),
            hit_col.astype(jnp.bfloat16),
            (((1,), (1,)), ((), ())),
            preferred_element_type=jnp.float32,
        )
    row = lax.broadcasted_iota(jnp.int32, (rows, LANES), 0)
    label = jnp.zeros((rows, LANES), jnp.int32)
    for c in range(blocks):
        label = jnp.where((row & (blocks - 1)) == c, int_label_ref[c ^ grp], label)
    odd = (label + amp_label_ref[...]) & 1
    weight = jnp.where(odd == 1, -counts, counts)
    col = lax.broadcasted_iota(jnp.int32, (rows, LANES), 1)
    follow = jnp.where(counts > 0.5, col, LANES)
    step = 1
    while step < amp_dev:
        follow = jnp.minimum(follow, pltpu.roll(follow, LANES - step, 1))
        step *= 2
    return weight, follow


def product_kernel(
    lanes,
    blocks,
    owner_ref,
    int_label_ref,
    lists_ref,
    amp_label_ref,
    amp_ref,
    *rest,
):
    int_refs = rest[:blocks]
    out_ref, weight_v, follow_v, weight_s, follow_s, st_hi, st_lo, in_hi, in_lo, sems = rest[blocks:]
    amp_dev, tile_rows, depth = amp_ref.shape
    weight, follow = coefficients(
        lists_ref, amp_label_ref, owner_ref, int_label_ref, amp_dev, lanes, blocks
    )
    weight_v[...] = weight
    follow_v[...] = follow
    one = pltpu.make_async_copy(weight_v, weight_s, sems.at[0])
    two = pltpu.make_async_copy(follow_v, follow_s, sems.at[1])
    one.start()
    two.start()
    for c in range(blocks):
        hi, lo = split(int_refs[c][...])
        in_hi[c] = hi
        in_lo[c] = lo
    one.wait()
    two.wait()

    def stack(s, _):
        def more(carry):
            return carry[0] < amp_dev

        def add(carry):
            a, total = carry
            return follow_s[s, a + 1], total + weight_s[s, a] * amp_ref[a]

        _, total = lax.while_loop(
            more, add, (follow_s[s, 0], jnp.zeros((tile_rows, depth), jnp.float32))
        )
        hi, lo = split(total)
        st_hi[s] = hi
        st_lo[s] = lo
        return 0

    lax.fori_loop(0, lanes * blocks, stack, 0)
    group = max(1, 256 // tile_rows)
    for p in range(0, lanes, group):
        total = None
        for c in range(blocks):
            pick = [(p + q) * blocks + c for q in range(group)]
            hi = jnp.concatenate([st_hi[s] for s in pick], 0)
            lo = jnp.concatenate([st_lo[s] for s in pick], 0)
            part = (
                jnp.dot(hi, in_hi[c], preferred_element_type=jnp.float32)
                + jnp.dot(hi, in_lo[c], preferred_element_type=jnp.float32)
                + jnp.dot(lo, in_hi[c], preferred_element_type=jnp.float32)
            )
            total = part if total is None else total + part
        out_ref[p : p + group] = total.reshape(group, tile_rows, total.shape[1])


def products(owner, int_label, lists, amp_label, amplitudes, ints, lanes):
    blocks = len(ints)
    amp_dev, tile_rows, depth = amplitudes.shape
    window = ints[0].shape[1]
    rows = lanes * blocks
    smem = pl.BlockSpec(memory_space=pltpu.SMEM)
    vmem = pl.BlockSpec(memory_space=pltpu.VMEM)
    return pl.pallas_call(
        functools.partial(product_kernel, lanes, blocks),
        out_shape=jax.ShapeDtypeStruct((lanes, tile_rows, window), jnp.float32),
        in_specs=[smem, smem, vmem, vmem, vmem] + [vmem] * blocks,
        out_specs=vmem,
        scratch_shapes=[
            pltpu.VMEM((rows, LANES), jnp.float32),
            pltpu.VMEM((rows, LANES), jnp.int32),
            pltpu.SMEM((rows, LANES), jnp.float32),
            pltpu.SMEM((rows, LANES), jnp.int32),
            pltpu.VMEM((rows, tile_rows, depth), jnp.bfloat16),
            pltpu.VMEM((rows, tile_rows, depth), jnp.bfloat16),
            pltpu.VMEM((blocks, depth, window), jnp.bfloat16),
            pltpu.VMEM((blocks, depth, window), jnp.bfloat16),
            pltpu.SemaphoreType.DMA((2,)),
        ],
        compiler_params=pltpu.CompilerParams(vmem_limit_bytes=48 * 1024 * 1024),
        cost_estimate=pl.CostEstimate(
            flops=6 * lanes * tile_rows * blocks * depth * window,
            bytes_accessed=amplitudes.size * 4 + blocks * depth * window * 4,
            transcendentals=0,
        ),
        name="products",
    )(owner, int_label, lists, amp_label, amplitudes, *ints)


def on_device(
    amplitudes,
    integrals,
    base_residual,
    occ_gap,
    virt_sum,
    task_amp,
    task_int,
    task_res,
    task_count,
    res_owner,
    amp_label,
    int_label,
):
    lanes = lax.axis_size("wide")
    grps = lax.axis_size("grp")
    slots = task_amp.shape[1]
    ints = [integrals] + [None] * (grps - 1)
    for k in range(2, grps, 2):
        ints[k] = swap(integrals, "grp", k)
    ints[1] = swap(integrals, "grp", 1)
    for k in range(2, grps, 2):
        ints[k + 1] = swap(ints[k], "grp", 1)
    lists = jnp.stack(
        [task_amp, task_int, task_res, jnp.broadcast_to(task_count[:, None], (1, slots))]
    )
    k = 1
    while k < lanes:
        lists = jnp.concatenate([lists, swap(lists, "wide", k)], axis=1)
        k *= 2
    labels = jnp.pad(amp_label, (0, LANES - amp_label.shape[0]))[None, :]
    image = products(
        res_owner, int_label, lists, labels, amplitudes, [x[0] for x in ints], lanes
    )
    far = list(range(lanes - 2, lanes // 2 - 1, -2))
    near = list(range(lanes // 2 - 2, -1, -2))
    total = {}
    for part in (far, near):
        got = swap(jnp.concatenate([image[k + 1 : k + 2] for k in part], 0), "wide", 1)
        for i, k in enumerate(part):
            total[k] = image[k : k + 1] + got[i : i + 1]
    summed = base_residual + total[0]
    for k in far + near:
        if k:
            summed = summed + swap(total[k], "wide", k)
    divisor = occ_gap[:, :, None] + virt_sum[None, None, :]
    return summed / divisor


def solution(mesh):
    return jax.shard_map(
        on_device,
        mesh=mesh,
        in_specs=(
            P(("grp", "wide"), None, None),
            P("grp", None, None),
            P(("grp", "wide"), None, None),
            P(("grp", "wide"), None),
            P(),
            P(("grp", "wide"), None),
            P(("grp", "wide"), None),
            P(("grp", "wide"), None),
            P(("grp", "wide")),
            P("grp", None),
            P(("grp", "wide")),
            P(),
        ),
        out_specs=P(("grp", "wide"), None, None),
        check_vma=False,
    )
```

```python
import functools

import jax
import jax.numpy as jnp
from jax import lax
from jax.experimental import pallas as pl
from jax.experimental.pallas import tpu as pltpu
from jax.sharding import PartitionSpec as P

LANES = 128
MIB = 1024 * 1024
VMEM = pl.BlockSpec(memory_space=pltpu.VMEM)


def split(x):
    hi = x.astype(jnp.bfloat16)
    return hi, (x - hi.astype(jnp.float32)).astype(jnp.bfloat16)


def swap(x, axis, k):
    n = lax.axis_size(axis)
    return lax.ppermute(x, axis, [(i, i ^ k) for i in range(n)])


def after(x, *others):
    return lax.optimization_barrier((x, *others))[0]


def tile_order(lanes):
    side = list(range(lanes // 2, lanes, 2)) + list(range(lanes // 2 - 2, -1, -2))
    return [k + 1 for k in side], side


def quarter_ids(lane):
    low = lane & 1
    side = low ^ ((lane >> 1) & 1)
    return (2 * side + low, 2 * side + 1 - low, 3 - 2 * side - low, 2 - 2 * side + low)


def coefficients(lists_ref, table_ref, amp_dev, lanes, blocks):
    lane = lax.axis_index("wide")
    grp = lax.axis_index("grp")
    amp, cint, res, count = (lists_ref[i] for i in range(4))
    slot = lax.broadcasted_iota(jnp.int32, amp.shape, 1)
    local = amp - lane * amp_dev
    valid = (slot < count) & (local >= 0) & (local < amp_dev)
    away, side = tile_order(lanes)
    pos = jnp.zeros_like(res)
    for p in range(lanes):
        pos = jnp.where(res == table_ref[1:2, p : p + 1], p, pos)
    offset = pos ^ lane
    place = jnp.zeros_like(res)
    for j, k in enumerate(away + side):
        place = jnp.where(offset == k, j, place)
    seg = jnp.where(valid, place * blocks + (cint ^ grp), -1)
    rows = lanes * blocks
    row_id = lax.broadcasted_iota(jnp.int32, (rows, amp.shape[1]), 0)
    col_id = lax.broadcasted_iota(jnp.int32, (LANES, amp.shape[1]), 0)
    counts = jnp.zeros((rows, LANES), jnp.float32)
    for src in range(lanes):
        hit_row = jnp.where(row_id == seg[src : src + 1, :], 1.0, 0.0)
        hit_col = jnp.where(col_id == local[src : src + 1, :], 1.0, 0.0)
        counts += lax.dot_general(
            hit_row.astype(jnp.bfloat16),
            hit_col.astype(jnp.bfloat16),
            (((1,), (1,)), ((), ())),
            preferred_element_type=jnp.float32,
        )
    row = lax.broadcasted_iota(jnp.int32, (rows, LANES), 0)
    block = (row & (blocks - 1)) ^ grp
    label = jnp.zeros((rows, LANES), jnp.int32)
    for c in range(blocks):
        label = jnp.where(block == c, table_ref[2:3, c : c + 1], label)
    odd = (label + table_ref[0:1, :]) & 1
    weight = jnp.where(odd == 1, -counts, counts)
    col = lax.broadcasted_iota(jnp.int32, (rows, LANES), 1)
    follow = jnp.where(counts > 0.5, col, LANES)
    step = 1
    while step < amp_dev:
        follow = jnp.minimum(follow, pltpu.roll(follow, LANES - step, 1))
        step *= 2
    return weight, follow


def passes(st_hi, st_lo, in_hi, in_lo, first, count):
    hi = st_hi[first : first + count, :]
    lo = st_lo[first : first + count, :]
    dot = functools.partial(jnp.dot, preferred_element_type=jnp.float32)
    return dot(hi, in_hi[...]) + dot(hi, in_lo[...]) + dot(lo, in_hi[...])


def store_tiles(refs, out):
    tile_rows = refs[0].shape[1]
    for i, ref in enumerate(refs):
        ref[0] = out[i * tile_rows : (i + 1) * tile_rows]


def load_kernel(amp_hbm, amp_ref, sems):
    n = sems.shape[0]
    step = amp_ref.shape[0] // n
    copies = [
        pltpu.make_async_copy(
            amp_hbm.at[pl.ds(i * step, step)], amp_ref.at[pl.ds(i * step, step)], sems.at[i]
        )
        for i in range(n)
    ]
    for copy in copies:
        copy.start()
    for copy in copies:
        copy.wait()


def load(amplitudes):
    size = amplitudes.size * 4
    return pl.pallas_call(
        load_kernel,
        out_shape=pltpu.VMEM(amplitudes.shape, amplitudes.dtype),
        in_specs=[pl.BlockSpec(memory_space=pltpu.HBM)],
        out_specs=VMEM,
        scratch_shapes=[pltpu.SemaphoreType.DMA((4,))],
        compiler_params=pltpu.CompilerParams(vmem_limit_bytes=size + MIB),
        cost_estimate=pl.CostEstimate(flops=0, bytes_accessed=2 * size, transcendentals=0),
        name="load_amplitudes",
    )(pltpu.with_memory_space_constraint(amplitudes, pltpu.HBM))


def sums_kernel(lanes, blocks, lists_ref, table_ref, amp_ref, *rest):
    whole, parts = rest[:2], rest[2 : 2 + 4 * (blocks - 2)]
    rest = rest[2 + 4 * (blocks - 2) :]
    away = lanes // 2
    away_refs, rest = rest[:away], rest[away:]
    st_hi, st_lo, in_hi, in_lo, weight_v, follow_v, weight_s, follow_s, sems = rest
    amp_dev, tile_rows, depth = amp_ref.shape
    weight, follow = coefficients(lists_ref, table_ref, amp_dev, lanes, blocks)
    weight_v[...] = weight
    follow_v[...] = follow
    one = pltpu.make_async_copy(weight_v, weight_s, sems.at[0])
    two = pltpu.make_async_copy(follow_v, follow_s, sems.at[1])
    one.start()
    two.start()
    for c in range(2):
        hi, lo = split(whole[c][...])
        in_hi[c * depth : (c + 1) * depth, :] = hi
        in_lo[c * depth : (c + 1) * depth, :] = lo
    ids = quarter_ids(lax.axis_index("wide"))
    quarter = depth // 4
    for c in range(2, blocks):
        for i in range(4):
            hi, lo = split(parts[4 * (c - 2) + i][...])
            at = pl.ds(pl.multiple_of(c * depth + ids[i] * quarter, quarter), quarter)
            in_hi[at, :] = hi
            in_lo[at, :] = lo
    one.wait()
    two.wait()

    def stack(j, _):
        for c in range(blocks):
            s = j * blocks + c

            def more(carry):
                return carry[0] < amp_dev

            def add(carry, s=s):
                a, total = carry
                return follow_s[s, a + 1], total + weight_s[s, a] * amp_ref[a]

            _, total = lax.while_loop(
                more, add, (follow_s[s, 0], jnp.zeros((tile_rows, depth), jnp.float32))
            )
            hi, lo = split(total)
            at = pl.ds(pl.multiple_of(j * tile_rows, tile_rows), tile_rows)
            st_hi[at, c * depth : (c + 1) * depth] = hi
            st_lo[at, c * depth : (c + 1) * depth] = lo
        return 0

    lax.fori_loop(0, lanes, stack, 0)
    store_tiles(away_refs, passes(st_hi, st_lo, in_hi, in_lo, 0, away * tile_rows))


def side_kernel(st_hi, st_lo, in_hi, in_lo, *side_refs):
    rows = len(side_refs) * side_refs[0].shape[1]
    store_tiles(side_refs, passes(st_hi, st_lo, in_hi, in_lo, rows, rows))


def products(lists, table, amplitudes, whole, parts, lanes):
    blocks = 2 + len(parts)
    amp_dev, tile_rows, depth = amplitudes.shape
    window = whole[0].shape[1]
    rows = lanes * blocks
    half = lanes // 2
    tiles = [jax.ShapeDtypeStruct((1, tile_rows, window), jnp.float32)] * half
    packed_shapes = [pltpu.VMEM((lanes * tile_rows, blocks * depth), jnp.bfloat16)] * 2 + [
        pltpu.VMEM((blocks * depth, window), jnp.bfloat16)
    ] * 2
    packed_bytes = 4 * (lanes * tile_rows + window) * blocks * depth
    tile_bytes = half * tile_rows * window * 4
    int_bytes = 4 * blocks * depth * window

    cost = pl.CostEstimate(
        flops=3 * lanes * tile_rows * blocks * depth * window,
        bytes_accessed=packed_bytes,
        transcendentals=0,
    )

    out = pl.pallas_call(
        functools.partial(sums_kernel, lanes, blocks),
        out_shape=tiles + packed_shapes,
        in_specs=[VMEM] * (5 + 4 * len(parts)),
        out_specs=[VMEM] * (half + 4),
        scratch_shapes=[
            pltpu.VMEM((rows, LANES), jnp.float32),
            pltpu.VMEM((rows, LANES), jnp.int32),
            pltpu.SMEM((rows, LANES), jnp.float32),
            pltpu.SMEM((rows, LANES), jnp.int32),
            pltpu.SemaphoreType.DMA((2,)),
        ],
        compiler_params=pltpu.CompilerParams(
            vmem_limit_bytes=min(56 * MIB, int_bytes + 2 * tile_bytes + 8 * MIB)
        ),
        cost_estimate=cost,
        name="sums_and_away_products",
    )(lists, table, amplitudes, *whole, *[x for four in parts for x in four])
    away, packed = out[:half], out[half:]
    packed = [pltpu.with_memory_space_constraint(x, pltpu.VMEM) for x in packed]
    side = pl.pallas_call(
        side_kernel,
        out_shape=tiles,
        in_specs=[VMEM] * 4,
        out_specs=[VMEM] * half,
        compiler_params=pltpu.CompilerParams(vmem_limit_bytes=2 * tile_bytes + 8 * MIB),
        cost_estimate=cost,
        name="side_products",
    )(*packed)
    return away, side


def on_device(
    amplitudes,
    integrals,
    base_residual,
    occ_gap,
    virt_sum,
    task_amp,
    task_int,
    task_res,
    task_count,
    res_owner,
    amp_label,
    int_label,
):
    lanes = lax.axis_size("wide")
    grps = lax.axis_size("grp")
    slots = task_amp.shape[1]
    own = integrals[0]
    quarter = own.shape[0] // 4
    ids = quarter_ids(lax.axis_index("wide"))
    send = [lax.dynamic_slice_in_dim(own, ids[i] * quarter, quarter, 0) for i in range(2)]
    fetched = {k: [swap(x, "grp", k) for x in send] for k in range(2, grps, 2)}
    whole = [own, swap(own, "grp", 1)]

    lists = jnp.stack(
        [task_amp, task_int, task_res, jnp.broadcast_to(task_count[:, None], (1, slots))]
    )
    amplitudes = load(amplitudes)
    k = 1
    while k < lanes:
        lists = jnp.concatenate([lists, swap(lists, "wide", k)], axis=1)
        if k == 1:
            lists = early = after(lists, amplitudes)
        k *= 2
    table = jnp.stack(
        [jnp.pad(x, (0, LANES - x.shape[0])) for x in (amp_label, res_owner[0], int_label)]
    )

    parts = [None] * (grps - 2)
    for k, (one, two) in fetched.items():
        relay = after(one, early)
        four = [one, two, swap(relay, "wide", 1), swap(relay, "wide", 2)]
        parts[k - 2] = four
        parts[k - 1] = [swap(after(x, lists), "grp", 1) for x in four]

    amplitudes = pltpu.with_memory_space_constraint(amplitudes, pltpu.VMEM)
    away, mine = products(lists, table, amplitudes, whole, parts, lanes)
    _, offsets = tile_order(lanes)
    got = [swap(x, "wide", 1) for x in away]
    summed = base_residual
    for k, here, there in zip(offsets, mine, got):
        part = here + there
        summed = summed + (swap(part, "wide", k) if k else part)
    divisor = occ_gap[:, :, None] + virt_sum[None, None, :]
    return summed / divisor


def solution(mesh):
    return jax.shard_map(
        on_device,
        mesh=mesh,
        in_specs=(
            P(("grp", "wide"), None, None),
            P("grp", None, None),
            P(("grp", "wide"), None, None),
            P(("grp", "wide"), None),
            P(),
            P(("grp", "wide"), None),
            P(("grp", "wide"), None),
            P(("grp", "wide"), None),
            P(("grp", "wide")),
            P("grp", None),
            P(("grp", "wide")),
            P(),
        ),
        out_specs=P(("grp", "wide"), None, None),
        check_vma=False,
    )
```

```python
import functools

import jax
import jax.numpy as jnp
from jax import lax
from jax.experimental import pallas as pl
from jax.experimental.pallas import tpu as pltpu
from jax.sharding import PartitionSpec as P

LANES = 128
MIB = 1024 * 1024
VMEM = pl.BlockSpec(memory_space=pltpu.VMEM)


def split(x):
    hi = x.astype(jnp.bfloat16)
    return hi, (x - hi.astype(jnp.float32)).astype(jnp.bfloat16)


def swap(x, axis, k):
    n = lax.axis_size(axis)
    return lax.ppermute(x, axis, [(i, i ^ k) for i in range(n)])


def after(x, *others):
    return lax.optimization_barrier((x, *others))[0]


def tile_order(lanes):
    side = list(range(lanes // 2, lanes, 2)) + list(range(lanes // 2 - 2, -1, -2))
    return [k + 1 for k in side], side


def row_cuts(depth):
    end = depth * 9 // 32 // 16 * 16
    return end, depth - 2 * end


def end_offsets(depth):
    low = lax.axis_index("wide") & 1
    last = depth - row_cuts(depth)[0]
    return pl.multiple_of(low * last, 16), pl.multiple_of(last - low * last, 16)


def prepare_kernel(*refs):
    count_ref, small, own_hbm = refs[0], refs[1:7], refs[7]
    one_ref, two_ref, lists_ref, table_ref = refs[8:12]
    (amp, cint, res, amp_label, owner, int_label), sems = refs[12:18], refs[18]
    end, middle = one_ref.shape[0], two_ref.shape[0]
    mine, _ = end_offsets(own_hbm.shape[0])
    moves = list(zip(small, refs[12:18]))
    moves.append((own_hbm.at[pl.ds(mine, end), :], one_ref))
    moves.append((own_hbm.at[pl.ds(end, middle), :], two_ref))
    copies = [pltpu.make_async_copy(a, b, sems.at[i]) for i, (a, b) in enumerate(moves)]
    for copy in copies:
        copy.start()
    table_ref[...] = jnp.zeros(table_ref.shape, jnp.int32)
    for copy in copies:
        copy.wait()
    slot = lax.broadcasted_iota(jnp.int32, amp.shape, 1)
    lists_ref[0] = amp[...]
    lists_ref[1] = cint[...]
    lists_ref[2] = jnp.where(slot < count_ref[0], res[...], -1)
    for i, ref in enumerate((amp_label, owner, int_label)):
        table_ref[i : i + 1, 0 : ref.shape[1]] = ref[...]


def prepare(task_amp, task_int, task_res, task_count, amp_label, owner, int_label, own):
    pieces = [pltpu.VMEM((n, own.shape[1]), own.dtype) for n in row_cuts(own.shape[0])]
    args = [task_amp, task_int, task_res, amp_label[None, :], owner, int_label[None, :], own]
    return pl.pallas_call(
        prepare_kernel,
        out_shape=[
            *pieces,
            pltpu.VMEM((3,) + task_amp.shape, jnp.int32),
            pltpu.VMEM((3, LANES), jnp.int32),
        ],
        in_specs=[pl.BlockSpec(memory_space=pltpu.SMEM)] + [pl.BlockSpec(memory_space=pltpu.HBM)] * 7,
        out_specs=[VMEM] * 4,
        scratch_shapes=[pltpu.VMEM(x.shape, x.dtype) for x in args[:6]]
        + [pltpu.SemaphoreType.DMA((8,))],
        compiler_params=pltpu.CompilerParams(vmem_limit_bytes=8 * MIB),
        cost_estimate=pl.CostEstimate(flops=0, bytes_accessed=own.size * 4, transcendentals=0),
        name="prepare",
    )(task_count, *[pltpu.with_memory_space_constraint(x, pltpu.HBM) for x in args])


def load_kernel(amp_hbm, amp_ref, sems):
    n = sems.shape[0]
    step = amp_ref.shape[0] // n
    copies = [
        pltpu.make_async_copy(
            amp_hbm.at[pl.ds(i * step, step)], amp_ref.at[pl.ds(i * step, step)], sems.at[i]
        )
        for i in range(n)
    ]
    for copy in copies:
        copy.start()
    for copy in copies:
        copy.wait()


def load(amplitudes):
    size = amplitudes.size * 4
    return pl.pallas_call(
        load_kernel,
        out_shape=pltpu.VMEM(amplitudes.shape, amplitudes.dtype),
        in_specs=[pl.BlockSpec(memory_space=pltpu.HBM)],
        out_specs=VMEM,
        scratch_shapes=[pltpu.SemaphoreType.DMA((4,))],
        compiler_params=pltpu.CompilerParams(vmem_limit_bytes=size + MIB),
        cost_estimate=pl.CostEstimate(flops=0, bytes_accessed=2 * size, transcendentals=0),
        name="load_amplitudes",
    )(pltpu.with_memory_space_constraint(amplitudes, pltpu.HBM))


def coefficients(lists_ref, table_ref, amp_dev, lanes, blocks):
    lane = lax.axis_index("wide")
    grp = lax.axis_index("grp")
    amp, cint, res = (lists_ref[i] for i in range(3))
    local = amp - lane * amp_dev
    valid = (res >= 0) & (local >= 0) & (local < amp_dev)
    away, side = tile_order(lanes)
    pos = jnp.zeros_like(res)
    for p in range(lanes):
        pos = jnp.where(res == table_ref[1:2, p : p + 1], p, pos)
    offset = pos ^ lane
    place = jnp.zeros_like(res)
    for j, k in enumerate(away + side):
        place = jnp.where(offset == k, j, place)
    seg = jnp.where(valid, place * blocks + (cint ^ grp), -1)
    rows = lanes * blocks
    row_id = lax.broadcasted_iota(jnp.int32, (rows, amp.shape[1]), 0)
    col_id = lax.broadcasted_iota(jnp.int32, (LANES, amp.shape[1]), 0)
    counts = jnp.zeros((rows, LANES), jnp.float32)
    for src in range(lanes):
        hit_row = jnp.where(row_id == seg[src : src + 1, :], 1.0, 0.0)
        hit_col = jnp.where(col_id == local[src : src + 1, :], 1.0, 0.0)
        counts += lax.dot_general(
            hit_row.astype(jnp.bfloat16),
            hit_col.astype(jnp.bfloat16),
            (((1,), (1,)), ((), ())),
            preferred_element_type=jnp.float32,
        )
    row = lax.broadcasted_iota(jnp.int32, (rows, LANES), 0)
    block = (row & (blocks - 1)) ^ grp
    label = jnp.zeros((rows, LANES), jnp.int32)
    for c in range(blocks):
        label = jnp.where(block == c, table_ref[2:3, c : c + 1], label)
    odd = (label + table_ref[0:1, :]) & 1
    weight = jnp.where(odd == 1, -counts, counts)
    col = lax.broadcasted_iota(jnp.int32, (rows, LANES), 1)
    follow = jnp.where(counts > 0.5, col, LANES)
    step = 1
    while step < amp_dev:
        follow = jnp.minimum(follow, pltpu.roll(follow, LANES - step, 1))
        step *= 2
    return weight, follow


def passes(hi, lo, in_hi, in_lo):
    dot = functools.partial(jnp.dot, preferred_element_type=jnp.float32)
    return dot(hi, in_hi[...]) + dot(hi, in_lo[...]) + dot(lo, in_hi[...])


def sums_kernel(lanes, blocks, lists_ref, table_ref, amp_ref, *rest):
    st_hi, st_lo, weight_v, follow_v, weight_s, follow_s, sems = rest
    amp_dev, tile_rows, depth = amp_ref.shape
    weight, follow = coefficients(lists_ref, table_ref, amp_dev, lanes, blocks)
    weight_v[...] = weight
    follow_v[...] = follow
    moves = [
        pltpu.make_async_copy(weight_v, weight_s, sems.at[0]),
        pltpu.make_async_copy(follow_v, follow_s, sems.at[1]),
    ]
    for copy in moves:
        copy.start()
    for copy in moves:
        copy.wait()

    def stack(j, _):
        for c in range(blocks):
            s = j * blocks + c

            def more(carry):
                return carry[0] < amp_dev

            def add(carry, s=s):
                a, total = carry
                return follow_s[s, a + 1], total + weight_s[s, a] * amp_ref[a]

            _, total = lax.while_loop(
                more, add, (follow_s[s, 0], jnp.zeros((tile_rows, depth), jnp.float32))
            )
            hi, lo = split(total)
            at = pl.ds(pl.multiple_of(j * tile_rows, tile_rows), tile_rows)
            st_hi[at, c * depth : (c + 1) * depth] = hi
            st_lo[at, c * depth : (c + 1) * depth] = lo
        return 0

    lax.fori_loop(0, lanes, stack, 0)


def local_kernel(st_hi, st_lo, own_ref, pair_ref, local_ref, in_hi, in_lo):
    depth = own_ref.shape[0]
    for c, ref in enumerate((own_ref, pair_ref)):
        hi, lo = split(ref[...])
        in_hi[c * depth : (c + 1) * depth, :] = hi
        in_lo[c * depth : (c + 1) * depth, :] = lo
    local_ref[...] = passes(st_hi[:, : 2 * depth], st_lo[:, : 2 * depth], in_hi, in_lo)


def add_remote(st_hi, st_lo, local_ref, in_hi, in_lo, first, out_refs):
    tile_rows = out_refs[0].shape[1]
    remote = in_hi.shape[0]
    at = slice(first * tile_rows, (first + len(out_refs)) * tile_rows)
    lead = st_hi.shape[1] - remote
    out = local_ref[at, :] + passes(st_hi[at, lead:], st_lo[at, lead:], in_hi, in_lo)
    for i, ref in enumerate(out_refs):
        ref[0] = out[i * tile_rows : (i + 1) * tile_rows]


def first_kernel(blocks, st_hi, st_lo, local_ref, *rest):
    parts, rest = rest[: 3 * (blocks - 2)], rest[3 * (blocks - 2) :]
    out_refs, (in_hi, in_lo) = rest[:-2], rest[-2:]
    depth = in_hi.shape[0] // (blocks - 2)
    mine, theirs = end_offsets(depth)
    for c in range(blocks - 2):
        starts = (mine, row_cuts(depth)[0], theirs)
        for start, part in zip(starts, parts[3 * c : 3 * c + 3]):
            hi, lo = split(part[...])
            at = pl.ds(pl.multiple_of(c * depth + start, 16), part.shape[0])
            in_hi[at, :] = hi
            in_lo[at, :] = lo
    add_remote(st_hi, st_lo, local_ref, in_hi, in_lo, 0, out_refs)


def second_kernel(first, st_hi, st_lo, local_ref, in_hi, in_lo, *out_refs):
    add_remote(st_hi, st_lo, local_ref, in_hi, in_lo, first, out_refs)


def limit(n):
    return pltpu.CompilerParams(vmem_limit_bytes=min(n + 12 * MIB, 56 * MIB))


def sums(lists, table, amplitudes, lanes, blocks):
    amp_dev, tile_rows, depth = amplitudes.shape
    rows = lanes * blocks
    held = pltpu.VMEM((lanes * tile_rows, blocks * depth), jnp.bfloat16)
    return pl.pallas_call(
        functools.partial(sums_kernel, lanes, blocks),
        out_shape=[held, held],
        in_specs=[VMEM] * 3,
        out_specs=[VMEM] * 2,
        scratch_shapes=[
            pltpu.VMEM((rows, LANES), jnp.float32),
            pltpu.VMEM((rows, LANES), jnp.int32),
            pltpu.SMEM((rows, LANES), jnp.float32),
            pltpu.SMEM((rows, LANES), jnp.int32),
            pltpu.SemaphoreType.DMA((2,)),
        ],
        compiler_params=limit(amplitudes.size * 4),
        cost_estimate=pl.CostEstimate(
            flops=0, bytes_accessed=4 * amplitudes.size, transcendentals=0
        ),
        name="sums",
    )(lists, table, pltpu.with_memory_space_constraint(amplitudes, pltpu.VMEM))


def local_products(held, own, pair):
    depth, window = own.shape
    rows = held[0].shape[0]
    half = pltpu.VMEM((2 * depth, window), jnp.bfloat16)
    return pl.pallas_call(
        local_kernel,
        out_shape=pltpu.VMEM((rows, window), jnp.float32),
        in_specs=[VMEM] * 4,
        out_specs=VMEM,
        scratch_shapes=[half, half],
        compiler_params=limit(16 * depth * window),
        cost_estimate=pl.CostEstimate(
            flops=12 * rows * depth * window, bytes_accessed=0, transcendentals=0
        ),
        name="local_products",
    )(*[pltpu.with_memory_space_constraint(x, pltpu.VMEM) for x in held], own, pair)


def add_products(held, parts, lanes, tile_rows):
    blocks = 2 + len(parts)
    depth = held[0].shape[1] // blocks
    window = held[2].shape[1]
    tile = jax.ShapeDtypeStruct((1, tile_rows, window), jnp.float32)
    remote = pltpu.VMEM(((blocks - 2) * depth, window), jnp.bfloat16)
    first = lanes // 2 + 1
    held = [pltpu.with_memory_space_constraint(x, pltpu.VMEM) for x in held]

    def cost(n):
        return pl.CostEstimate(
            flops=6 * n * tile_rows * (blocks - 2) * depth * window,
            bytes_accessed=4 * n * tile_rows * window,
            transcendentals=0,
        )

    *tiles, in_hi, in_lo = pl.pallas_call(
        functools.partial(first_kernel, blocks),
        out_shape=[tile] * first + [remote] * 2,
        in_specs=[VMEM] * (3 + 3 * len(parts)),
        out_specs=[VMEM] * (first + 2),
        compiler_params=limit(4 * blocks * depth * window),
        cost_estimate=cost(first),
        name="first_products",
    )(*held, *[x for three in parts for x in three])
    packed = [pltpu.with_memory_space_constraint(x, pltpu.VMEM) for x in (in_hi, in_lo)]
    others = pl.pallas_call(
        functools.partial(second_kernel, first),
        out_shape=[tile] * (lanes - first),
        in_specs=[VMEM] * 5,
        out_specs=[VMEM] * (lanes - first),
        compiler_params=limit(0),
        cost_estimate=cost(lanes - first),
        name="second_products",
    )(*held, *packed)
    return [*tiles, *others]


def on_device(
    amplitudes,
    integrals,
    base_residual,
    occ_gap,
    virt_sum,
    task_amp,
    task_int,
    task_res,
    task_count,
    res_owner,
    amp_label,
    int_label,
):
    lanes = lax.axis_size("wide")
    grps = lax.axis_size("grp")
    own = integrals[0]
    one, two, lists, table = prepare(
        task_amp, task_int, task_res, task_count, amp_label, res_owner, int_label, own
    )
    fetched = {k: [swap(x, "grp", k) for x in (one, two)] for k in range(2, grps, 2)}
    amplitudes = load(amplitudes)
    k = 1
    while k < lanes:
        if k == 2:
            lists = after(lists, amplitudes)
        lists = jnp.concatenate([lists, swap(lists, "wide", k)], axis=1)
        k *= 2
    pair = swap(own, "grp", 1)
    held = sums(lists, table, amplitudes, lanes, grps)

    parts = [None] * (grps - 2)
    for k, (one, two) in fetched.items():
        three = [one, two, swap(one, "wide", 1)]
        parts[k - 2] = three
        parts[k - 1] = [swap(after(x, y), "grp", 1) for x, y in zip(three, (lists, held[0], held[0]))]

    held = [*held, local_products(held, own, pair)]
    tiles = add_products(held, parts, lanes, amplitudes.shape[1])
    _, offsets = tile_order(lanes)
    got = [swap(x, "wide", 1) for x in tiles[: lanes // 2]]
    summed = base_residual
    for k, here, there in zip(offsets, tiles[lanes // 2 :], got):
        part = here + there
        summed = summed + (swap(part, "wide", k) if k else part)
    divisor = occ_gap[:, :, None] + virt_sum[None, None, :]
    return summed / divisor


def solution(mesh):
    return jax.shard_map(
        on_device,
        mesh=mesh,
        in_specs=(
            P(("grp", "wide"), None, None),
            P("grp", None, None),
            P(("grp", "wide"), None, None),
            P(("grp", "wide"), None),
            P(),
            P(("grp", "wide"), None),
            P(("grp", "wide"), None),
            P(("grp", "wide"), None),
            P(("grp", "wide")),
            P("grp", None),
            P(("grp", "wide")),
            P(),
        ),
        out_specs=P(("grp", "wide"), None, None),
        check_vma=False,
    )
```

```python
import functools

import jax
import jax.numpy as jnp
from jax import lax
from jax.experimental import pallas as pl
from jax.experimental.pallas import tpu as pltpu
from jax.sharding import PartitionSpec as P

LANES = 128
MIB = 1024 * 1024
DEEP = 256
VMEM = pl.BlockSpec(memory_space=pltpu.VMEM)
HBM = pl.BlockSpec(memory_space=pltpu.HBM)


def in_vmem(x):
    return pltpu.with_memory_space_constraint(x, pltpu.VMEM)


def in_hbm(x):
    return pltpu.with_memory_space_constraint(x, pltpu.HBM)


def limit(n):
    return pltpu.CompilerParams(vmem_limit_bytes=min(n + 12 * MIB, 56 * MIB))


def cost(flops, nbytes):
    return pl.CostEstimate(flops=flops, bytes_accessed=nbytes, transcendentals=0)


def split(x):
    hi = x.astype(jnp.bfloat16)
    return hi, (x - hi.astype(jnp.float32)).astype(jnp.bfloat16)


def swap(x, axis, k):
    n = lax.axis_size(axis)
    return lax.ppermute(x, axis, [(i, i ^ k) for i in range(n)])


def after(x, *others):
    return lax.optimization_barrier((x, *others))[0]


def tile_order(lanes):
    side = list(range(lanes // 2, lanes, 2)) + list(range(lanes // 2 - 2, -1, -2))
    return [k + 1 for k in side], side


def row_cuts(depth):
    end = depth * 9 // 32 // 16 * 16
    return end, depth - 2 * end


def end_offsets(depth):
    low = lax.axis_index("wide") & 1
    last = depth - row_cuts(depth)[0]
    return pl.multiple_of(low * last, 16), pl.multiple_of(last - low * last, 16)


def pieces_kernel(own_hbm, one_ref, two_ref, sems):
    end, middle = one_ref.shape[0], two_ref.shape[0]
    mine, _ = end_offsets(own_hbm.shape[0])
    copies = [
        pltpu.make_async_copy(own_hbm.at[pl.ds(mine, end), :], one_ref, sems.at[0]),
        pltpu.make_async_copy(own_hbm.at[pl.ds(end, middle), :], two_ref, sems.at[1]),
    ]
    for copy in copies:
        copy.start()
    for copy in copies:
        copy.wait()


def pieces(own):
    return pl.pallas_call(
        pieces_kernel,
        out_shape=[pltpu.VMEM((n, own.shape[1]), own.dtype) for n in row_cuts(own.shape[0])],
        in_specs=[HBM],
        out_specs=[VMEM] * 2,
        scratch_shapes=[pltpu.SemaphoreType.DMA((2,))],
        compiler_params=limit(0),
        cost_estimate=cost(0, own.size * 4),
        name="pieces",
    )(in_hbm(own))


def lists_kernel(count_ref, *refs):
    small, (lists_ref, table_ref) = refs[:6], refs[6:8]
    held, sems = refs[8:14], refs[14]
    amp, cint, res, amp_label, owner, int_label = held
    copies = [pltpu.make_async_copy(a, b, sems.at[i]) for i, (a, b) in enumerate(zip(small, held))]
    for copy in copies:
        copy.start()
    table_ref[...] = jnp.zeros(table_ref.shape, jnp.int32)
    for copy in copies:
        copy.wait()
    slot = lax.broadcasted_iota(jnp.int32, amp.shape, 1)
    lists_ref[0] = amp[...]
    lists_ref[1] = cint[...]
    lists_ref[2] = jnp.where(slot < count_ref[0], res[...], -1)
    amp_dev = amp_label.shape[1]
    for at in range(0, DEEP, amp_dev):
        table_ref[0:1, at : at + amp_dev] = amp_label[...]
    table_ref[1:2, 0 : owner.shape[1]] = owner[...]
    table_ref[2:3, 0 : int_label.shape[1]] = int_label[...]


def pack_lists(task_amp, task_int, task_res, task_count, amp_label, owner, int_label):
    args = [task_amp, task_int, task_res, amp_label[None, :], owner, int_label[None, :]]
    return pl.pallas_call(
        lists_kernel,
        out_shape=[
            pltpu.VMEM((3,) + task_amp.shape, jnp.int32),
            pltpu.VMEM((3, DEEP), jnp.int32),
        ],
        in_specs=[pl.BlockSpec(memory_space=pltpu.SMEM)] + [HBM] * 6,
        out_specs=[VMEM] * 2,
        scratch_shapes=[pltpu.VMEM(x.shape, x.dtype) for x in args]
        + [pltpu.SemaphoreType.DMA((6,))],
        compiler_params=limit(0),
        cost_estimate=cost(0, 4096),
        name="pack_lists",
    )(task_count, *[in_hbm(x) for x in args])


def load_kernel(first, amp_hbm, out_ref, rows_ref, sems):
    amp_dev = amp_hbm.shape[0]
    rows = rows_ref.shape[0]
    copies = [
        pltpu.make_async_copy(amp_hbm.at[:, first + i, :], rows_ref.at[i], sems.at[i])
        for i in range(rows)
    ]
    for copy in copies:
        copy.start()
    for i, copy in enumerate(copies):
        copy.wait()
        hi, lo = split(rows_ref[i])
        at = 2 * amp_dev * i
        out_ref[at : at + amp_dev, :] = hi
        out_ref[at + amp_dev : at + 2 * amp_dev, :] = lo


def load(amplitudes, first, rows):
    amp_dev, _, depth = amplitudes.shape
    return pl.pallas_call(
        functools.partial(load_kernel, first),
        out_shape=pltpu.VMEM((rows * 2 * amp_dev, depth), jnp.bfloat16),
        in_specs=[HBM],
        out_specs=VMEM,
        scratch_shapes=[
            pltpu.VMEM((rows, amp_dev, depth), jnp.float32),
            pltpu.SemaphoreType.DMA((rows,)),
        ],
        compiler_params=limit(8 * rows * amp_dev * depth),
        cost_estimate=cost(0, 8 * rows * amp_dev * depth),
        name="load_amplitudes",
    )(in_hbm(amplitudes))


def local_kernel(own_ref, pair_ref, in_hi, in_lo):
    depth = own_ref.shape[0]
    for c, ref in enumerate((own_ref, pair_ref)):
        hi, lo = split(ref[...])
        in_hi[c * depth : (c + 1) * depth, :] = hi
        in_lo[c * depth : (c + 1) * depth, :] = lo


def split_local(own, pair):
    depth, window = own.shape
    return pl.pallas_call(
        local_kernel,
        out_shape=[pltpu.VMEM((2 * depth, window), jnp.bfloat16)] * 2,
        in_specs=[VMEM] * 2,
        out_specs=[VMEM] * 2,
        compiler_params=limit(16 * depth * window),
        cost_estimate=cost(0, 16 * depth * window),
        name="split_local",
    )(own, pair)


def coefficients(lists_ref, table_ref, amp_dev, lanes, blocks):
    lane = lax.axis_index("wide")
    grp = lax.axis_index("grp")
    amp, cint, res = (lists_ref[i] for i in range(3))
    local = amp - lane * amp_dev
    valid = (res >= 0) & (local >= 0) & (local < amp_dev)
    pos = jnp.zeros_like(res)
    for p in range(lanes):
        pos = jnp.where(res == table_ref[1:2, p : p + 1], p, pos)
    offset = pos ^ lane
    place = jnp.zeros_like(res)
    away, side = tile_order(lanes)
    for j, k in enumerate(away + side):
        place = jnp.where(offset == k, j, place)
    seg = jnp.where(valid, place * blocks + (cint ^ grp), -1)
    half = lanes // 2
    group = DEEP // (2 * amp_dev)
    rows = 2 * blocks * group * half
    slots = amp.shape[1]

    def parts(row):
        tile = row & (half - 1)
        inner = (row >> (half.bit_length() - 1)) & (group - 1)
        outer = row >> ((half * group).bit_length() - 1)
        return tile, inner, outer & (blocks - 1), outer >> (blocks.bit_length() - 1)

    tile, _, block, away_or_side = parts(lax.broadcasted_iota(jnp.int32, (rows, slots), 0))
    row_seg = (away_or_side * half + tile) * blocks + block
    col_amp = lax.broadcasted_iota(jnp.int32, (DEEP, slots), 0) & (amp_dev - 1)
    counts = jnp.zeros((rows, DEEP), jnp.float32)
    for src in range(lanes):
        hit_row = jnp.where(row_seg == seg[src : src + 1, :], 1.0, 0.0)
        hit_col = jnp.where(col_amp == local[src : src + 1, :], 1.0, 0.0)
        counts += lax.dot_general(
            hit_row.astype(jnp.bfloat16),
            hit_col.astype(jnp.bfloat16),
            (((1,), (1,)), ((), ())),
            preferred_element_type=jnp.float32,
        )
    _, inner, block, _ = parts(lax.broadcasted_iota(jnp.int32, (rows, DEEP), 0))
    block = block ^ grp
    label = jnp.zeros((rows, DEEP), jnp.int32)
    for c in range(blocks):
        label = jnp.where(block == c, table_ref[2:3, c : c + 1], label)
    odd = (label + table_ref[0:1, :]) & 1
    col = lax.broadcasted_iota(jnp.int32, (rows, DEEP), 1)
    same = inner == (col >> ((2 * amp_dev).bit_length() - 1))
    weight = jnp.where(odd == 1, -counts, counts)
    return jnp.where(same, weight, 0.0).astype(jnp.bfloat16)


def sums_kernel(lanes, blocks, amp_dev, lists_ref, table_ref, *refs):
    amp_refs, sums_refs = refs[:-4], refs[-4:]
    weight = coefficients(lists_ref, table_ref, amp_dev, lanes, blocks)
    depth = amp_refs[0].shape[1]
    step = weight.shape[0] // (2 * blocks)
    first = 0
    for ref in amp_refs:
        count = ref.shape[0] // DEEP

        def add(g, _, ref=ref, first=first):
            rows = ref[pl.ds(pl.multiple_of(g * DEEP, DEEP), DEEP), :]
            total = jnp.dot(weight, rows, preferred_element_type=jnp.float32)
            at = pl.ds(pl.multiple_of((first + g) * step, step), step)
            for k in range(2):
                for c in range(blocks):
                    r = (k * blocks + c) * step
                    hi, lo = split(total[r : r + step, :])
                    sums_refs[2 * k][at, c * depth : (c + 1) * depth] = hi
                    sums_refs[2 * k + 1][at, c * depth : (c + 1) * depth] = lo
            return 0

        lax.fori_loop(0, count, add, 0)
        first += count


def sums(lists, table, rows, amp_dev, tile_rows, lanes, blocks):
    depth = rows[0].shape[1]
    held = pltpu.VMEM((lanes // 2 * tile_rows, blocks * depth), jnp.bfloat16)
    return pl.pallas_call(
        functools.partial(sums_kernel, lanes, blocks, amp_dev),
        out_shape=[held] * 4,
        in_specs=[VMEM] * (2 + len(rows)),
        out_specs=[VMEM] * 4,
        compiler_params=limit(0),
        cost_estimate=cost(0, 16 * tile_rows * amp_dev * depth),
        name="sums",
    )(lists, table, *[in_vmem(x) for x in rows])


def passes(hi, lo, in_hi, in_lo):
    dot = functools.partial(jnp.dot, preferred_element_type=jnp.float32)
    return dot(hi, in_hi) + dot(hi, in_lo) + dot(lo, in_hi)


def store_tiles(out, out_refs, held):
    tiles = len(out_refs)
    rows = out.shape[0] // tiles
    for b in range(held.shape[0]):
        held[b] = out[:, b * LANES : (b + 1) * LANES]
    for j, ref in enumerate(out_refs):
        for b in range(held.shape[0]):
            ref[0, :, b * LANES : (b + 1) * LANES] = held[b, pl.ds(j, rows, stride=tiles), :]


def local_products_kernel(hi, lo, in_hi, in_lo, out_ref):
    depth = in_hi.shape[0]
    out_ref[...] = passes(hi[:, :depth], lo[:, :depth], in_hi[...], in_lo[...])


def local_products(hi, lo, in_hi, in_lo):
    depth, window = in_hi.shape
    return pl.pallas_call(
        local_products_kernel,
        out_shape=pltpu.VMEM((hi.shape[0], window), jnp.float32),
        in_specs=[VMEM] * 4,
        out_specs=VMEM,
        compiler_params=limit(0),
        cost_estimate=cost(6 * hi.shape[0] * depth * window, 0),
        name="local_products",
    )(*[in_vmem(x) for x in (hi, lo, in_hi, in_lo)])


def away_kernel(tiles, blocks, hi, lo, local_ref, *rest):
    n = 3 * (blocks - 2)
    parts, out_refs, (in_hi, in_lo, held) = rest[:n], rest[n : n + tiles], rest[n + tiles :]
    depth = in_hi.shape[0] // (blocks - 2)
    mine, theirs = end_offsets(depth)
    for c in range(blocks - 2):
        starts = (mine, row_cuts(depth)[0], theirs)
        for start, part in zip(starts, parts[3 * c : 3 * c + 3]):
            high, low = split(part[...])
            at = pl.ds(pl.multiple_of(c * depth + start, 16), part.shape[0])
            in_hi[at, :] = high
            in_lo[at, :] = low
    out = passes(hi[:, 2 * depth :], lo[:, 2 * depth :], in_hi[...], in_lo[...])
    store_tiles(local_ref[...] + out, out_refs, held)


def side_kernel(tiles, hi, lo, local_hi, local_lo, in_hi, in_lo, *rest):
    out_refs, held = rest[:tiles], rest[tiles]
    depth = local_hi.shape[0]
    out = passes(hi[:, :depth], lo[:, :depth], local_hi[...], local_lo[...])
    out += passes(hi[:, depth:], lo[:, depth:], in_hi[...], in_lo[...])
    store_tiles(out, out_refs, held)


def away_products(hi, lo, local, parts, tiles):
    blocks = 2 + len(parts)
    depth = hi.shape[1] // blocks
    rows, window = local.shape
    remote = pltpu.VMEM(((blocks - 2) * depth, window), jnp.bfloat16)
    *out, in_hi, in_lo = pl.pallas_call(
        functools.partial(away_kernel, tiles, blocks),
        out_shape=[jax.ShapeDtypeStruct((1, rows // tiles, window), jnp.float32)] * tiles
        + [remote] * 2,
        in_specs=[VMEM] * (3 + 3 * len(parts)),
        out_specs=[VMEM] * (tiles + 2),
        scratch_shapes=[pltpu.VMEM((window // LANES, rows, LANES), jnp.float32)],
        compiler_params=limit(4 * blocks * depth * window),
        cost_estimate=cost(6 * rows * (blocks - 2) * depth * window, 0),
        name="away_products",
    )(*[in_vmem(x) for x in (hi, lo, local)], *[x for three in parts for x in three])
    return out, in_hi, in_lo


def side_products(hi, lo, local_hi, local_lo, in_hi, in_lo, tiles):
    rows, depth = hi.shape
    window = in_hi.shape[1]
    return pl.pallas_call(
        functools.partial(side_kernel, tiles),
        out_shape=[jax.ShapeDtypeStruct((1, rows // tiles, window), jnp.float32)] * tiles,
        in_specs=[VMEM] * 6,
        out_specs=[VMEM] * tiles,
        scratch_shapes=[pltpu.VMEM((window // LANES, rows, LANES), jnp.float32)],
        compiler_params=limit(0),
        cost_estimate=cost(6 * rows * depth * window, 0),
        name="side_products",
    )(*[in_vmem(x) for x in (hi, lo, local_hi, local_lo, in_hi, in_lo)])


def on_device(
    amplitudes,
    integrals,
    base_residual,
    occ_gap,
    virt_sum,
    task_amp,
    task_int,
    task_res,
    task_count,
    res_owner,
    amp_label,
    int_label,
):
    lanes = lax.axis_size("wide")
    grps = lax.axis_size("grp")
    amp_dev, tile_rows, _ = amplitudes.shape
    half = lanes // 2
    own = integrals[0]
    one, two = pieces(own)
    fetched = {k: [swap(x, "grp", k) for x in (one, two)] for k in range(2, grps, 2)}
    lists, table = pack_lists(
        task_amp, task_int, after(task_res, one), task_count, amp_label, res_owner, int_label
    )
    pair = swap(own, "grp", 1)
    rows = [load(amplitudes, i * tile_rows // 2, tile_rows // 2) for i in range(2)]
    local_hi, local_lo = split_local(own, pair)
    k = 1
    while k < lanes:
        if k in (2, 4):
            lists = after(lists, rows[k // 4])
        lists = jnp.concatenate([lists, swap(lists, "wide", k)], axis=1)
        k *= 2
    away_hi, away_lo, side_hi, side_lo = sums(lists, table, rows, amp_dev, tile_rows, lanes, grps)

    parts = [None] * (grps - 2)
    for k, (one, two) in fetched.items():
        three = [one, two, swap(one, "wide", 1)]
        parts[k - 2] = three
        parts[k - 1] = [
            swap(after(x, y), "grp", 1) for x, y in zip(three, (lists, away_hi, away_hi))
        ]

    local = local_products(away_hi, away_lo, local_hi, local_lo)
    away, in_hi, in_lo = away_products(away_hi, away_lo, local, parts, half)
    side = side_products(side_hi, side_lo, local_hi, local_lo, in_hi, in_lo, half)
    _, offsets = tile_order(lanes)
    got = [swap(x, "wide", 1) for x in away]
    summed = base_residual
    for k, here, there in reversed(list(zip(offsets, side, got))):
        part = here + there
        summed = summed + (swap(part, "wide", k) if k else part)
    divisor = occ_gap[:, :, None] + virt_sum[None, None, :]
    return summed / divisor


def solution(mesh):
    return jax.shard_map(
        on_device,
        mesh=mesh,
        in_specs=(
            P(("grp", "wide"), None, None),
            P("grp", None, None),
            P(("grp", "wide"), None, None),
            P(("grp", "wide"), None),
            P(),
            P(("grp", "wide"), None),
            P(("grp", "wide"), None),
            P(("grp", "wide"), None),
            P(("grp", "wide")),
            P("grp", None),
            P(("grp", "wide")),
            P(),
        ),
        out_specs=P(("grp", "wide"), None, None),
        check_vma=False,
    )
```

```python
import functools

import jax
import jax.numpy as jnp
from jax import lax
from jax.experimental import pallas as pl
from jax.experimental.pallas import tpu as pltpu
from jax.sharding import PartitionSpec as P

LANES = 128
MIB = 1024 * 1024
DEEP = 256
VMEM = pl.BlockSpec(memory_space=pltpu.VMEM)
HBM = pl.BlockSpec(memory_space=pltpu.HBM)


def in_vmem(x):
    return pltpu.with_memory_space_constraint(x, pltpu.VMEM)


def in_hbm(x):
    return pltpu.with_memory_space_constraint(x, pltpu.HBM)


def limit(n):
    return pltpu.CompilerParams(vmem_limit_bytes=min(n + 12 * MIB, 56 * MIB))


def cost(flops, nbytes):
    return pl.CostEstimate(flops=flops, bytes_accessed=nbytes, transcendentals=0)


def split(x):
    hi = x.astype(jnp.bfloat16)
    return hi, (x - hi.astype(jnp.float32)).astype(jnp.bfloat16)


def swap(x, axis, k):
    n = lax.axis_size(axis)
    return lax.ppermute(x, axis, [(i, i ^ k) for i in range(n)])


def after(x, *others):
    return lax.optimization_barrier((x, *others))[0]


def tile_order(lanes):
    side = list(range(lanes // 2, lanes, 2)) + list(range(lanes // 2 - 2, -1, -2))
    return [k + 1 for k in side], side


def row_cuts(depth):
    end = depth * 9 // 32 // 16 * 16
    return end, depth - 2 * end


def end_offsets(depth):
    low = lax.axis_index("wide") & 1
    last = depth - row_cuts(depth)[0]
    return pl.multiple_of(low * last, 16), pl.multiple_of(last - low * last, 16)


def pieces_kernel(own_hbm, one_ref, two_ref, sems):
    end, middle = one_ref.shape[0], two_ref.shape[0]
    mine, _ = end_offsets(own_hbm.shape[0])
    copies = [
        pltpu.make_async_copy(own_hbm.at[pl.ds(mine, end), :], one_ref, sems.at[0]),
        pltpu.make_async_copy(own_hbm.at[pl.ds(end, middle), :], two_ref, sems.at[1]),
    ]
    for copy in copies:
        copy.start()
    for copy in copies:
        copy.wait()


def pieces(own):
    return pl.pallas_call(
        pieces_kernel,
        out_shape=[pltpu.VMEM((n, own.shape[1]), own.dtype) for n in row_cuts(own.shape[0])],
        in_specs=[HBM],
        out_specs=[VMEM] * 2,
        scratch_shapes=[pltpu.SemaphoreType.DMA((2,))],
        compiler_params=limit(0),
        cost_estimate=cost(0, own.size * 4),
        name="pieces",
    )(in_hbm(own))


def lists_kernel(count_ref, *refs):
    small, (lists_ref, table_ref) = refs[:6], refs[6:8]
    held, sems = refs[8:14], refs[14]
    amp, cint, res, amp_label, owner, int_label = held
    copies = [pltpu.make_async_copy(a, b, sems.at[i]) for i, (a, b) in enumerate(zip(small, held))]
    for copy in copies:
        copy.start()
    table_ref[...] = jnp.zeros(table_ref.shape, jnp.int32)
    for copy in copies:
        copy.wait()
    slot = lax.broadcasted_iota(jnp.int32, amp.shape, 1)
    lists_ref[0] = amp[...]
    lists_ref[1] = cint[...]
    lists_ref[2] = jnp.where(slot < count_ref[0], res[...], -1)
    amp_dev = amp_label.shape[1]
    for at in range(0, DEEP, amp_dev):
        table_ref[0:1, at : at + amp_dev] = amp_label[...]
    table_ref[1:2, 0 : owner.shape[1]] = owner[...]
    table_ref[2:3, 0 : int_label.shape[1]] = int_label[...]


def pack_lists(task_amp, task_int, task_res, task_count, amp_label, owner, int_label):
    args = [task_amp, task_int, task_res, amp_label[None, :], owner, int_label[None, :]]
    return pl.pallas_call(
        lists_kernel,
        out_shape=[
            pltpu.VMEM((3,) + task_amp.shape, jnp.int32),
            pltpu.VMEM((3, DEEP), jnp.int32),
        ],
        in_specs=[pl.BlockSpec(memory_space=pltpu.SMEM)] + [HBM] * 6,
        out_specs=[VMEM] * 2,
        scratch_shapes=[pltpu.VMEM(x.shape, x.dtype) for x in args]
        + [pltpu.SemaphoreType.DMA((6,))],
        compiler_params=limit(0),
        cost_estimate=cost(0, 4096),
        name="pack_lists",
    )(task_count, *[in_hbm(x) for x in args])


def load_kernel(first, amp_hbm, out_ref, rows_ref, sems):
    amp_dev = amp_hbm.shape[0]
    rows = rows_ref.shape[0]
    copies = [
        pltpu.make_async_copy(amp_hbm.at[:, first + i, :], rows_ref.at[i], sems.at[i])
        for i in range(rows)
    ]
    for copy in copies:
        copy.start()
    for i, copy in enumerate(copies):
        copy.wait()
        hi, lo = split(rows_ref[i])
        at = 2 * amp_dev * i
        out_ref[at : at + amp_dev, :] = hi
        out_ref[at + amp_dev : at + 2 * amp_dev, :] = lo


def load(amplitudes, first, rows):
    amp_dev, _, depth = amplitudes.shape
    return pl.pallas_call(
        functools.partial(load_kernel, first),
        out_shape=pltpu.VMEM((rows * 2 * amp_dev, depth), jnp.bfloat16),
        in_specs=[HBM],
        out_specs=VMEM,
        scratch_shapes=[
            pltpu.VMEM((rows, amp_dev, depth), jnp.float32),
            pltpu.SemaphoreType.DMA((rows,)),
        ],
        compiler_params=limit(8 * rows * amp_dev * depth),
        cost_estimate=cost(0, 8 * rows * amp_dev * depth),
        name="load_amplitudes",
    )(in_hbm(amplitudes))


def coefficients(lists_ref, table_ref, amp_dev, lanes, blocks):
    lane = lax.axis_index("wide")
    grp = lax.axis_index("grp")
    amp, cint, res = (lists_ref[i] for i in range(3))
    local = amp - lane * amp_dev
    valid = (res >= 0) & (local >= 0) & (local < amp_dev)
    pos = jnp.zeros_like(res)
    for p in range(lanes):
        pos = jnp.where(res == table_ref[1:2, p : p + 1], p, pos)
    offset = pos ^ lane
    place = jnp.zeros_like(res)
    away, side = tile_order(lanes)
    for j, k in enumerate(away + side):
        place = jnp.where(offset == k, j, place)
    seg = jnp.where(valid, place * blocks + (cint ^ grp), -1)
    half = lanes // 2
    group = DEEP // (2 * amp_dev)
    rows = 2 * blocks * group * half
    slots = amp.shape[1]

    def parts(row):
        tile = row & (half - 1)
        inner = (row >> (half.bit_length() - 1)) & (group - 1)
        outer = row >> ((half * group).bit_length() - 1)
        return tile, inner, outer & (blocks - 1), outer >> (blocks.bit_length() - 1)

    tile, _, block, away_or_side = parts(lax.broadcasted_iota(jnp.int32, (rows, slots), 0))
    row_seg = (away_or_side * half + tile) * blocks + block
    col_amp = lax.broadcasted_iota(jnp.int32, (DEEP, slots), 0) & (amp_dev - 1)
    counts = jnp.zeros((rows, DEEP), jnp.float32)
    for src in range(lanes):
        hit_row = jnp.where(row_seg == seg[src : src + 1, :], 1.0, 0.0)
        hit_col = jnp.where(col_amp == local[src : src + 1, :], 1.0, 0.0)
        counts += lax.dot_general(
            hit_row.astype(jnp.bfloat16),
            hit_col.astype(jnp.bfloat16),
            (((1,), (1,)), ((), ())),
            preferred_element_type=jnp.float32,
        )
    _, inner, block, _ = parts(lax.broadcasted_iota(jnp.int32, (rows, DEEP), 0))
    block = block ^ grp
    label = jnp.zeros((rows, DEEP), jnp.int32)
    for c in range(blocks):
        label = jnp.where(block == c, table_ref[2:3, c : c + 1], label)
    odd = (label + table_ref[0:1, :]) & 1
    col = lax.broadcasted_iota(jnp.int32, (rows, DEEP), 1)
    same = inner == (col >> ((2 * amp_dev).bit_length() - 1))
    weight = jnp.where(odd == 1, -counts, counts)
    return jnp.where(same, weight, 0.0).astype(jnp.bfloat16)


def passes(hi, lo, in_hi, in_lo):
    dot = functools.partial(jnp.dot, preferred_element_type=jnp.float32)
    return dot(hi, in_hi) + dot(hi, in_lo) + dot(lo, in_hi)


def store_tiles(out, out_refs, held):
    tiles = len(out_refs)
    rows = out.shape[0] // tiles
    for b in range(held.shape[0]):
        held[b] = out[:, b * LANES : (b + 1) * LANES]
    for j, ref in enumerate(out_refs):
        for b in range(held.shape[0]):
            ref[0, :, b * LANES : (b + 1) * LANES] = held[b, pl.ds(j, rows, stride=tiles), :]


def sums_kernel(lanes, blocks, amp_dev, lists_ref, table_ref, own_ref, pair_ref, *refs):
    amp_refs, sums_refs, local_refs, (in_hi, in_lo) = refs[:2], refs[2:6], refs[6:8], refs[8:]
    weight = coefficients(lists_ref, table_ref, amp_dev, lanes, blocks)
    depth = own_ref.shape[0]
    step = weight.shape[0] // (2 * blocks)
    first = 0
    for ref in amp_refs:
        count = ref.shape[0] // DEEP
        for g in range(count):
            rows = ref[g * DEEP : (g + 1) * DEEP, :]
            total = jnp.dot(weight, rows, preferred_element_type=jnp.float32)
            at = slice((first + g) * step, (first + g + 1) * step)
            for k in range(2):
                for c in range(blocks):
                    r = (k * blocks + c) * step
                    hi, lo = split(total[r : r + step, :])
                    sums_refs[2 * k][at, c * depth : (c + 1) * depth] = hi
                    sums_refs[2 * k + 1][at, c * depth : (c + 1) * depth] = lo
        first += count
    for c, ref in enumerate((own_ref, pair_ref)):
        hi, lo = split(ref[...])
        in_hi[c * depth : (c + 1) * depth, :] = hi
        in_lo[c * depth : (c + 1) * depth, :] = lo
    for k, ref in enumerate(local_refs):
        hi, lo = (x[:, : 2 * depth] for x in sums_refs[2 * k : 2 * k + 2])
        ref[...] = passes(hi, lo, in_hi[...], in_lo[...])


def sums(lists, table, own, pair, rows, amp_dev, tile_rows, lanes, blocks):
    depth, window = own.shape
    kept = lanes // 2 * tile_rows
    held = pltpu.VMEM((kept, blocks * depth), jnp.bfloat16)
    local = pltpu.VMEM((2 * depth, window), jnp.bfloat16)
    product = pltpu.VMEM((kept, window), jnp.float32)
    return pl.pallas_call(
        functools.partial(sums_kernel, lanes, blocks, amp_dev),
        out_shape=[held] * 4 + [product] * 2,
        in_specs=[VMEM] * (4 + len(rows)),
        out_specs=[VMEM] * 6,
        scratch_shapes=[local] * 2,
        compiler_params=limit(16 * depth * window),
        cost_estimate=cost(0, 16 * tile_rows * amp_dev * depth),
        name="sums",
    )(lists, table, own, pair, *[in_vmem(x) for x in rows])


def away_kernel(blocks, hi, lo, local_ref, *rest):
    n = 3 * (blocks - 2)
    parts, out_refs, (in_hi, in_lo, held) = rest[:n], rest[n:-3], rest[-3:]
    depth = in_hi.shape[0] // (blocks - 2)
    mine, theirs = end_offsets(depth)
    for c in range(blocks - 2):
        starts = (mine, row_cuts(depth)[0], theirs)
        for start, part in zip(starts, parts[3 * c : 3 * c + 3]):
            high, low = split(part[...])
            at = pl.ds(pl.multiple_of(c * depth + start, 16), part.shape[0])
            in_hi[at, :] = high
            in_lo[at, :] = low
    out = passes(hi[:, 2 * depth :], lo[:, 2 * depth :], in_hi[...], in_lo[...])
    store_tiles(local_ref[...] + out, out_refs, held)


def side_kernel(hi, lo, local_ref, in_hi, in_lo, *rest):
    out_refs, held = rest[:-1], rest[-1]
    lead = hi.shape[1] - in_hi.shape[0]
    out = passes(hi[:, lead:], lo[:, lead:], in_hi[...], in_lo[...])
    store_tiles(local_ref[...] + out, out_refs, held)


def away_products(hi, lo, local, parts, tiles):
    blocks = 2 + len(parts)
    depth = hi.shape[1] // blocks
    rows, window = local.shape
    remote = pltpu.VMEM(((blocks - 2) * depth, window), jnp.bfloat16)
    shapes = [jax.ShapeDtypeStruct((1, rows // tiles, window), jnp.float32)] * tiles
    *out, in_hi, in_lo = pl.pallas_call(
        functools.partial(away_kernel, blocks),
        out_shape=shapes + [remote] * 2,
        in_specs=[VMEM] * (3 + 3 * len(parts)),
        out_specs=[VMEM] * (len(shapes) + 2),
        scratch_shapes=[pltpu.VMEM((window // LANES, rows, LANES), jnp.float32)],
        compiler_params=limit(4 * blocks * depth * window),
        cost_estimate=cost(6 * rows * (blocks - 2) * depth * window, 0),
        name="away_products",
    )(*[in_vmem(x) for x in (hi, lo, local)], *[x for three in parts for x in three])
    return out, in_hi, in_lo


def side_products(hi, lo, local, in_hi, in_lo, tiles):
    rows, window = local.shape
    shapes = [jax.ShapeDtypeStruct((1, rows // tiles, window), jnp.float32)] * tiles
    return pl.pallas_call(
        side_kernel,
        out_shape=shapes,
        in_specs=[VMEM] * 5,
        out_specs=[VMEM] * len(shapes),
        scratch_shapes=[pltpu.VMEM((window // LANES, rows, LANES), jnp.float32)],
        compiler_params=limit(0),
        cost_estimate=cost(6 * rows * in_hi.size, 0),
        name="side_products",
    )(*[in_vmem(x) for x in (hi, lo, local, in_hi, in_lo)])


def on_device(
    amplitudes,
    integrals,
    base_residual,
    occ_gap,
    virt_sum,
    task_amp,
    task_int,
    task_res,
    task_count,
    res_owner,
    amp_label,
    int_label,
):
    lanes = lax.axis_size("wide")
    grps = lax.axis_size("grp")
    amp_dev, tile_rows, _ = amplitudes.shape
    half = lanes // 2
    own = integrals[0]
    one, two = pieces(own)
    fetched = {k: [swap(x, "grp", k) for x in (one, two)] for k in range(2, grps, 2)}
    lists, table = pack_lists(
        task_amp, task_int, after(task_res, one), task_count, amp_label, res_owner, int_label
    )
    pair = swap(own, "grp", 1)
    rows = [load(amplitudes, i * tile_rows // 2, tile_rows // 2) for i in range(2)]
    k = 1
    while k < lanes:
        if k == 2:
            lists = after(lists, rows[0])
        lists = jnp.concatenate([lists, swap(lists, "wide", k)], axis=1)
        k *= 2
    lists = after(lists, rows[1])
    away_hi, away_lo, side_hi, side_lo, *local = sums(
        lists, table, own, pair, rows, amp_dev, tile_rows, lanes, grps
    )

    parts = [None] * (grps - 2)
    for k, (one, two) in fetched.items():
        three = [one, two, swap(one, "wide", 1)]
        parts[k - 2] = three
        parts[k - 1] = [
            swap(after(x, y), "grp", 1) for x, y in zip(three, (lists, away_hi, away_hi))
        ]

    away, in_hi, in_lo = away_products(away_hi, away_lo, local[0], parts, half)
    side = side_products(side_hi, side_lo, local[1], in_hi, in_lo, half)
    _, offsets = tile_order(lanes)
    got = [swap(x, "wide", 1) for x in away]
    summed = base_residual
    for k, here, there in zip(offsets, side, got):
        part = here + there
        summed = summed + (swap(part, "wide", k) if k else part)
    divisor = occ_gap[:, :, None] + virt_sum[None, None, :]
    return summed / divisor


def solution(mesh):
    return jax.shard_map(
        on_device,
        mesh=mesh,
        in_specs=(
            P(("grp", "wide"), None, None),
            P("grp", None, None),
            P(("grp", "wide"), None, None),
            P(("grp", "wide"), None),
            P(),
            P(("grp", "wide"), None),
            P(("grp", "wide"), None),
            P(("grp", "wide"), None),
            P(("grp", "wide")),
            P("grp", None),
            P(("grp", "wide")),
            P(),
        ),
        out_specs=P(("grp", "wide"), None, None),
        check_vma=False,
    )
```

```python
import functools

import jax
import jax.numpy as jnp
from jax import lax
from jax.experimental import pallas as pl
from jax.experimental.pallas import tpu as pltpu
from jax.sharding import PartitionSpec as P

LANES = 128
MIB = 1024 * 1024
DEEP = 256
VMEM = pl.BlockSpec(memory_space=pltpu.VMEM)
HBM = pl.BlockSpec(memory_space=pltpu.HBM)


def in_vmem(x):
    return pltpu.with_memory_space_constraint(x, pltpu.VMEM)


def in_hbm(x):
    return pltpu.with_memory_space_constraint(x, pltpu.HBM)


def limit(n):
    return pltpu.CompilerParams(vmem_limit_bytes=min(n + 12 * MIB, 56 * MIB))


def cost(flops, nbytes):
    return pl.CostEstimate(flops=flops, bytes_accessed=nbytes, transcendentals=0)


def split(x):
    hi = x.astype(jnp.bfloat16)
    return hi, (x - hi.astype(jnp.float32)).astype(jnp.bfloat16)


def swap(x, axis, k):
    n = lax.axis_size(axis)
    return lax.ppermute(x, axis, [(i, i ^ k) for i in range(n)])


def after(x, *others):
    return lax.optimization_barrier((x, *others))[0]


def tile_order(lanes):
    half = lanes // 2
    side = [half] + list(range(half - 2, 0, -2)) + list(range(half + 2, lanes, 2)) + [0]
    return [k + 1 for k in side], side


def row_cuts(depth):
    end = depth * 9 // 32 // 16 * 16
    return end, depth - 2 * end


def end_offsets(depth):
    low = lax.axis_index("wide") & 1
    last = depth - row_cuts(depth)[0]
    return pl.multiple_of(low * last, 16), pl.multiple_of(last - low * last, 16)


def pieces_kernel(own_hbm, one_ref, two_ref, sems):
    end, middle = one_ref.shape[0], two_ref.shape[0]
    mine, _ = end_offsets(own_hbm.shape[0])
    copies = [
        pltpu.make_async_copy(own_hbm.at[pl.ds(mine, end), :], one_ref, sems.at[0]),
        pltpu.make_async_copy(own_hbm.at[pl.ds(end, middle), :], two_ref, sems.at[1]),
    ]
    for copy in copies:
        copy.start()
    for copy in copies:
        copy.wait()


def pieces(own):
    return pl.pallas_call(
        pieces_kernel,
        out_shape=[pltpu.VMEM((n, own.shape[1]), own.dtype) for n in row_cuts(own.shape[0])],
        in_specs=[HBM],
        out_specs=[VMEM] * 2,
        scratch_shapes=[pltpu.SemaphoreType.DMA((2,))],
        compiler_params=limit(0),
        cost_estimate=cost(0, own.size * 4),
        name="pieces",
    )(in_hbm(own))


def lists_kernel(count_ref, *refs):
    small, (lists_ref, table_ref) = refs[:6], refs[6:8]
    held, sems = refs[8:14], refs[14]
    amp, cint, res, amp_label, owner, int_label = held
    copies = [pltpu.make_async_copy(a, b, sems.at[i]) for i, (a, b) in enumerate(zip(small, held))]
    for copy in copies:
        copy.start()
    table_ref[...] = jnp.zeros(table_ref.shape, jnp.int32)
    for copy in copies:
        copy.wait()
    slot = lax.broadcasted_iota(jnp.int32, amp.shape, 1)
    lists_ref[0] = amp[...]
    lists_ref[1] = cint[...]
    lists_ref[2] = jnp.where(slot < count_ref[0], res[...], -1)
    amp_dev = amp_label.shape[1]
    for at in range(0, DEEP, amp_dev):
        table_ref[0:1, at : at + amp_dev] = amp_label[...]
    table_ref[1:2, 0 : owner.shape[1]] = owner[...]
    table_ref[2:3, 0 : int_label.shape[1]] = int_label[...]


def pack_lists(task_amp, task_int, task_res, task_count, amp_label, owner, int_label):
    args = [task_amp, task_int, task_res, amp_label[None, :], owner, int_label[None, :]]
    return pl.pallas_call(
        lists_kernel,
        out_shape=[
            pltpu.VMEM((3,) + task_amp.shape, jnp.int32),
            pltpu.VMEM((3, DEEP), jnp.int32),
        ],
        in_specs=[pl.BlockSpec(memory_space=pltpu.SMEM)] + [HBM] * 6,
        out_specs=[VMEM] * 2,
        scratch_shapes=[pltpu.VMEM(x.shape, x.dtype) for x in args]
        + [pltpu.SemaphoreType.DMA((6,))],
        compiler_params=limit(0),
        cost_estimate=cost(0, 4096),
        name="pack_lists",
    )(task_count, *[in_hbm(x) for x in args])


def load_kernel(first, amp_hbm, out_ref, rows_ref, sems):
    amp_dev = amp_hbm.shape[0]
    rows = rows_ref.shape[0]
    copies = [
        pltpu.make_async_copy(amp_hbm.at[:, first + i, :], rows_ref.at[i], sems.at[i])
        for i in range(rows)
    ]
    for copy in copies:
        copy.start()
    for i, copy in enumerate(copies):
        copy.wait()
        hi, lo = split(rows_ref[i])
        at = 2 * amp_dev * i
        out_ref[at : at + amp_dev, :] = hi
        out_ref[at + amp_dev : at + 2 * amp_dev, :] = lo


def load(amplitudes, first, rows):
    amp_dev, _, depth = amplitudes.shape
    return pl.pallas_call(
        functools.partial(load_kernel, first),
        out_shape=pltpu.VMEM((rows * 2 * amp_dev, depth), jnp.bfloat16),
        in_specs=[HBM],
        out_specs=VMEM,
        scratch_shapes=[
            pltpu.VMEM((rows, amp_dev, depth), jnp.float32),
            pltpu.SemaphoreType.DMA((rows,)),
        ],
        compiler_params=limit(8 * rows * amp_dev * depth),
        cost_estimate=cost(0, 8 * rows * amp_dev * depth),
        name="load_amplitudes",
    )(in_hbm(amplitudes))


def coefficients(lists_ref, table_ref, amp_dev, lanes, blocks):
    lane = lax.axis_index("wide")
    grp = lax.axis_index("grp")
    amp, cint, res = (lists_ref[i] for i in range(3))
    local = amp - lane * amp_dev
    valid = (res >= 0) & (local >= 0) & (local < amp_dev)
    pos = jnp.zeros_like(res)
    for p in range(lanes):
        pos = jnp.where(res == table_ref[1:2, p : p + 1], p, pos)
    offset = pos ^ lane
    place = jnp.zeros_like(res)
    away, side = tile_order(lanes)
    for j, k in enumerate(away + side):
        place = jnp.where(offset == k, j, place)
    seg = jnp.where(valid, place * blocks + (cint ^ grp), -1)
    half = lanes // 2
    group = DEEP // (2 * amp_dev)
    rows = 2 * blocks * group * half
    slots = amp.shape[1]

    def parts(row):
        tile = row & (half - 1)
        inner = (row >> (half.bit_length() - 1)) & (group - 1)
        outer = row >> ((half * group).bit_length() - 1)
        return tile, inner, outer & (blocks - 1), outer >> (blocks.bit_length() - 1)

    tile, _, block, away_or_side = parts(lax.broadcasted_iota(jnp.int32, (rows, slots), 0))
    row_seg = (away_or_side * half + tile) * blocks + block
    col_amp = lax.broadcasted_iota(jnp.int32, (DEEP, slots), 0) & (amp_dev - 1)
    counts = jnp.zeros((rows, DEEP), jnp.float32)
    for src in range(lanes):
        hit_row = jnp.where(row_seg == seg[src : src + 1, :], 1.0, 0.0)
        hit_col = jnp.where(col_amp == local[src : src + 1, :], 1.0, 0.0)
        counts += lax.dot_general(
            hit_row.astype(jnp.bfloat16),
            hit_col.astype(jnp.bfloat16),
            (((1,), (1,)), ((), ())),
            preferred_element_type=jnp.float32,
        )
    _, inner, block, _ = parts(lax.broadcasted_iota(jnp.int32, (rows, DEEP), 0))
    block = block ^ grp
    label = jnp.zeros((rows, DEEP), jnp.int32)
    for c in range(blocks):
        label = jnp.where(block == c, table_ref[2:3, c : c + 1], label)
    odd = (label + table_ref[0:1, :]) & 1
    col = lax.broadcasted_iota(jnp.int32, (rows, DEEP), 1)
    same = inner == (col >> ((2 * amp_dev).bit_length() - 1))
    weight = jnp.where(odd == 1, -counts, counts)
    return jnp.where(same, weight, 0.0).astype(jnp.bfloat16)


def passes(hi, lo, in_hi, in_lo):
    dot = functools.partial(jnp.dot, preferred_element_type=jnp.float32)
    return dot(hi, in_hi) + dot(hi, in_lo) + dot(lo, in_hi)


def store_tiles(out, out_refs, held):
    tiles = len(out_refs)
    rows = out.shape[0] // tiles
    for b in range(held.shape[0]):
        held[b] = out[:, b * LANES : (b + 1) * LANES]
    for j, ref in enumerate(out_refs):
        for b in range(held.shape[0]):
            ref[0, :, b * LANES : (b + 1) * LANES] = held[b, pl.ds(j, rows, stride=tiles), :]


def sums_kernel(lanes, blocks, amp_dev, lists_ref, table_ref, own_ref, pair_ref, *refs):
    amp_refs, sums_refs, local_refs, (in_hi, in_lo) = refs[:2], refs[2:6], refs[6:8], refs[8:]
    weight = coefficients(lists_ref, table_ref, amp_dev, lanes, blocks)
    depth = own_ref.shape[0]
    step = weight.shape[0] // (2 * blocks)
    first = 0
    for ref in amp_refs:
        count = ref.shape[0] // DEEP
        for g in range(count):
            rows = ref[g * DEEP : (g + 1) * DEEP, :]
            total = jnp.dot(weight, rows, preferred_element_type=jnp.float32)
            at = slice((first + g) * step, (first + g + 1) * step)
            for k in range(2):
                for c in range(blocks):
                    r = (k * blocks + c) * step
                    hi, lo = split(total[r : r + step, :])
                    sums_refs[2 * k][at, c * depth : (c + 1) * depth] = hi
                    sums_refs[2 * k + 1][at, c * depth : (c + 1) * depth] = lo
        first += count
    for c, ref in enumerate((own_ref, pair_ref)):
        hi, lo = split(ref[...])
        in_hi[c * depth : (c + 1) * depth, :] = hi
        in_lo[c * depth : (c + 1) * depth, :] = lo
    for k, ref in enumerate(local_refs):
        hi, lo = (x[:, : 2 * depth] for x in sums_refs[2 * k : 2 * k + 2])
        ref[...] = passes(hi, lo, in_hi[...], in_lo[...])


def sums(lists, table, own, pair, rows, amp_dev, tile_rows, lanes, blocks):
    depth, window = own.shape
    kept = lanes // 2 * tile_rows
    held = pltpu.VMEM((kept, blocks * depth), jnp.bfloat16)
    local = pltpu.VMEM((2 * depth, window), jnp.bfloat16)
    product = pltpu.VMEM((kept, window), jnp.float32)
    return pl.pallas_call(
        functools.partial(sums_kernel, lanes, blocks, amp_dev),
        out_shape=[held] * 4 + [product] * 2,
        in_specs=[VMEM] * (4 + len(rows)),
        out_specs=[VMEM] * 6,
        scratch_shapes=[local] * 2,
        compiler_params=limit(16 * depth * window),
        cost_estimate=cost(0, 16 * tile_rows * amp_dev * depth),
        name="sums",
    )(lists, table, own, pair, *[in_vmem(x) for x in rows])


def split_parts(parts, in_hi, in_lo):
    depth = sum(x.shape[0] for x in parts[:3])
    mine, theirs = end_offsets(depth)
    for c in range(len(parts) // 3):
        starts = (mine, row_cuts(depth)[0], theirs)
        for start, part in zip(starts, parts[3 * c : 3 * c + 3]):
            hi, lo = split(part[...])
            at = pl.ds(pl.multiple_of(c * depth + start, 16), part.shape[0])
            in_hi[at, :] = hi
            in_lo[at, :] = lo


def columns(x, odd, depth):
    blocks = range(2 + odd, x.shape[1] // depth, 2)
    return jnp.concatenate([x[:, c * depth : (c + 1) * depth] for c in blocks], axis=1)


def fetched_kernel(*refs):
    sums_refs, local_refs, rest = refs[:4], refs[4:6], refs[6:]
    parts, out_refs, (in_hi, in_lo) = rest[:-4], rest[-4:-2], rest[-2:]
    depth = sum(x.shape[0] for x in parts[:3])
    split_parts(parts, in_hi, in_lo)
    for k in range(2):
        hi, lo = (columns(x, 0, depth) for x in sums_refs[2 * k : 2 * k + 2])
        out_refs[k][...] = local_refs[k][...] + passes(hi, lo, in_hi[...], in_lo[...])


def flat(parts):
    return [x for three in parts for x in three]


def fetched_products(held, local, parts):
    rows, window = local[0].shape
    depth = sum(x.shape[0] for x in parts[0])
    half = pltpu.VMEM((len(parts) * depth, window), jnp.bfloat16)
    return pl.pallas_call(
        fetched_kernel,
        out_shape=[pltpu.VMEM((rows, window), jnp.float32)] * 2,
        in_specs=[VMEM] * (6 + 3 * len(parts)),
        out_specs=[VMEM] * 2,
        scratch_shapes=[half] * 2,
        compiler_params=limit(16 * len(parts) * depth * window),
        cost_estimate=cost(12 * rows * len(parts) * depth * window, 0),
        name="fetched_products",
    )(*[in_vmem(x) for x in (*held, *local)], *flat(parts))


def away_kernel(tiles, hi, lo, local_ref, *rest):
    parts, out_refs, (in_hi, in_lo, held) = rest[: -3 - tiles], rest[-3 - tiles : -3], rest[-3:]
    split_parts(parts, in_hi, in_lo)
    depth = sum(x.shape[0] for x in parts[:3])
    out = passes(columns(hi, 1, depth), columns(lo, 1, depth), in_hi[...], in_lo[...])
    store_tiles(local_ref[...] + out, out_refs, held)


def side_kernel(depth, hi, lo, local_ref, in_hi, in_lo, *rest):
    out_refs, held = rest[:-1], rest[-1]
    out = passes(columns(hi, 1, depth), columns(lo, 1, depth), in_hi[...], in_lo[...])
    store_tiles(local_ref[...] + out, out_refs, held)


def away_products(hi, lo, local, parts, tiles):
    rows, window = local.shape
    depth = sum(x.shape[0] for x in parts[0])
    remote = pltpu.VMEM((len(parts) * depth, window), jnp.bfloat16)
    shapes = [jax.ShapeDtypeStruct((1, rows // tiles, window), jnp.float32)] * tiles
    *out, in_hi, in_lo = pl.pallas_call(
        functools.partial(away_kernel, tiles),
        out_shape=shapes + [remote] * 2,
        in_specs=[VMEM] * (3 + 3 * len(parts)),
        out_specs=[VMEM] * (tiles + 2),
        scratch_shapes=[pltpu.VMEM((window // LANES, rows, LANES), jnp.float32)],
        compiler_params=limit(16 * len(parts) * depth * window),
        cost_estimate=cost(6 * rows * len(parts) * depth * window, 0),
        name="away_products",
    )(*[in_vmem(x) for x in (hi, lo, local)], *flat(parts))
    return out, in_hi, in_lo


def side_products(hi, lo, local, in_hi, in_lo, tiles, depth):
    rows, window = local.shape
    shapes = [jax.ShapeDtypeStruct((1, rows // tiles, window), jnp.float32)] * tiles
    return pl.pallas_call(
        functools.partial(side_kernel, depth),
        out_shape=shapes,
        in_specs=[VMEM] * 5,
        out_specs=[VMEM] * tiles,
        scratch_shapes=[pltpu.VMEM((window // LANES, rows, LANES), jnp.float32)],
        compiler_params=limit(0),
        cost_estimate=cost(0, 0),
        name="side_products",
    )(*[in_vmem(x) for x in (hi, lo, local, in_hi, in_lo)])


def on_device(
    amplitudes,
    integrals,
    base_residual,
    occ_gap,
    virt_sum,
    task_amp,
    task_int,
    task_res,
    task_count,
    res_owner,
    amp_label,
    int_label,
):
    lanes = lax.axis_size("wide")
    grps = lax.axis_size("grp")
    amp_dev, tile_rows, _ = amplitudes.shape
    half = lanes // 2
    own = integrals[0]
    one, two = pieces(own)
    fetched = {k: [swap(x, "grp", k) for x in (one, two)] for k in range(2, grps, 2)}
    lists, table = pack_lists(
        task_amp, task_int, after(task_res, one), task_count, amp_label, res_owner, int_label
    )
    pair = swap(own, "grp", 1)
    rows = [load(amplitudes, i * tile_rows // 2, tile_rows // 2) for i in range(2)]
    k = 1
    while k < lanes:
        if k == 2:
            lists = after(lists, rows[0])
        lists = jnp.concatenate([lists, swap(lists, "wide", k)], axis=1)
        k *= 2
    lists = after(lists, rows[1])
    *held, local_away, local_side = sums(
        lists, table, own, pair, rows, amp_dev, tile_rows, lanes, grps
    )

    even, odd = [], []
    for k, (one, two) in fetched.items():
        even.append([one, two, swap(one, "wide", 1)])
        odd.append([swap(after(x, y), "grp", 1) for x, y in zip(even[-1], (lists, held[0], held[0]))])

    local = fetched_products(held, (local_away, local_side), even)
    away, in_hi, in_lo = away_products(*held[:2], local[0], odd, half)
    side = side_products(*held[2:], local[1], in_hi, in_lo, half, own.shape[0])
    _, offsets = tile_order(lanes)
    got = [swap(away[0], "wide", 1)]
    got += [swap(after(x, side[0]), "wide", 1) for x in away[1:]]
    summed = base_residual
    for k, here, there in zip(offsets, side, got):
        part = here + there
        summed = summed + (swap(part, "wide", k) if k else part)
    divisor = occ_gap[:, :, None] + virt_sum[None, None, :]
    return summed / divisor


def solution(mesh):
    return jax.shard_map(
        on_device,
        mesh=mesh,
        in_specs=(
            P(("grp", "wide"), None, None),
            P("grp", None, None),
            P(("grp", "wide"), None, None),
            P(("grp", "wide"), None),
            P(),
            P(("grp", "wide"), None),
            P(("grp", "wide"), None),
            P(("grp", "wide"), None),
            P(("grp", "wide")),
            P("grp", None),
            P(("grp", "wide")),
            P(),
        ),
        out_specs=P(("grp", "wide"), None, None),
        check_vma=False,
    )
```

```python
import functools

import jax
import jax.numpy as jnp
from jax import lax
from jax.experimental import pallas as pl
from jax.experimental.pallas import tpu as pltpu
from jax.sharding import PartitionSpec as P

LANES = 128
MIB = 1024 * 1024
DEEP = 256
VMEM = pl.BlockSpec(memory_space=pltpu.VMEM)
HBM = pl.BlockSpec(memory_space=pltpu.HBM)


def in_vmem(x):
    return pltpu.with_memory_space_constraint(x, pltpu.VMEM)


def in_hbm(x):
    return pltpu.with_memory_space_constraint(x, pltpu.HBM)


def limit(n):
    return pltpu.CompilerParams(vmem_limit_bytes=min(n + 12 * MIB, 56 * MIB))


def cost(flops, nbytes):
    return pl.CostEstimate(flops=flops, bytes_accessed=nbytes, transcendentals=0)


def split(x):
    hi = x.astype(jnp.bfloat16)
    return hi, (x - hi.astype(jnp.float32)).astype(jnp.bfloat16)


def swap(x, axis, k):
    n = lax.axis_size(axis)
    return lax.ppermute(x, axis, [(i, i ^ k) for i in range(n)])


def after(x, *others):
    return lax.optimization_barrier((x, *others))[0]


def tile_order(lanes):
    half = lanes // 2
    side = list(range(half, lanes, 2)) + list(range(half - 2, -1, -2))
    return [k + 1 for k in side], side


def row_cuts(depth):
    end = depth * 9 // 32 // 16 * 16
    return end, depth - 2 * end


def end_offsets(depth):
    low = lax.axis_index("wide") & 1
    last = depth - row_cuts(depth)[0]
    return pl.multiple_of(low * last, 16), pl.multiple_of(last - low * last, 16)


def pieces_kernel(own_hbm, one_ref, two_ref, sems):
    end, middle = one_ref.shape[0], two_ref.shape[0]
    mine, _ = end_offsets(own_hbm.shape[0])
    copies = [
        pltpu.make_async_copy(own_hbm.at[pl.ds(mine, end), :], one_ref, sems.at[0]),
        pltpu.make_async_copy(own_hbm.at[pl.ds(end, middle), :], two_ref, sems.at[1]),
    ]
    for copy in copies:
        copy.start()
    for copy in copies:
        copy.wait()


def pieces(own):
    return pl.pallas_call(
        pieces_kernel,
        out_shape=[pltpu.VMEM((n, own.shape[1]), own.dtype) for n in row_cuts(own.shape[0])],
        in_specs=[HBM],
        out_specs=[VMEM] * 2,
        scratch_shapes=[pltpu.SemaphoreType.DMA((2,))],
        compiler_params=limit(0),
        cost_estimate=cost(0, own.size * 4),
        name="pieces",
    )(in_hbm(own))


def lists_kernel(count_ref, *refs):
    small, (lists_ref, table_ref) = refs[:6], refs[6:8]
    held, sems = refs[8:14], refs[14]
    amp, cint, res, amp_label, owner, int_label = held
    copies = [pltpu.make_async_copy(a, b, sems.at[i]) for i, (a, b) in enumerate(zip(small, held))]
    for copy in copies:
        copy.start()
    table_ref[...] = jnp.zeros(table_ref.shape, jnp.int32)
    for copy in copies:
        copy.wait()
    slot = lax.broadcasted_iota(jnp.int32, amp.shape, 1)
    lists_ref[0] = amp[...]
    lists_ref[1] = cint[...]
    lists_ref[2] = jnp.where(slot < count_ref[0], res[...], -1)
    amp_dev = amp_label.shape[1]
    for at in range(0, DEEP, amp_dev):
        table_ref[0:1, at : at + amp_dev] = amp_label[...]
    table_ref[1:2, 0 : owner.shape[1]] = owner[...]
    table_ref[2:3, 0 : int_label.shape[1]] = int_label[...]


def pack_lists(task_amp, task_int, task_res, task_count, amp_label, owner, int_label):
    args = [task_amp, task_int, task_res, amp_label[None, :], owner, int_label[None, :]]
    return pl.pallas_call(
        lists_kernel,
        out_shape=[
            pltpu.VMEM((3,) + task_amp.shape, jnp.int32),
            pltpu.VMEM((3, DEEP), jnp.int32),
        ],
        in_specs=[pl.BlockSpec(memory_space=pltpu.SMEM)] + [HBM] * 6,
        out_specs=[VMEM] * 2,
        scratch_shapes=[pltpu.VMEM(x.shape, x.dtype) for x in args]
        + [pltpu.SemaphoreType.DMA((6,))],
        compiler_params=limit(0),
        cost_estimate=cost(0, 4096),
        name="pack_lists",
    )(task_count, *[in_hbm(x) for x in args])


def load_kernel(first, amp_hbm, out_ref, rows_ref, sems):
    amp_dev = amp_hbm.shape[0]
    rows = rows_ref.shape[0]
    copies = [
        pltpu.make_async_copy(amp_hbm.at[:, first + i, :], rows_ref.at[i], sems.at[i])
        for i in range(rows)
    ]
    for copy in copies:
        copy.start()
    for i, copy in enumerate(copies):
        copy.wait()
        hi, lo = split(rows_ref[i])
        at = 2 * amp_dev * i
        out_ref[at : at + amp_dev, :] = hi
        out_ref[at + amp_dev : at + 2 * amp_dev, :] = lo


def load(amplitudes, first, rows):
    amp_dev, _, depth = amplitudes.shape
    return pl.pallas_call(
        functools.partial(load_kernel, first),
        out_shape=pltpu.VMEM((rows * 2 * amp_dev, depth), jnp.bfloat16),
        in_specs=[HBM],
        out_specs=VMEM,
        scratch_shapes=[
            pltpu.VMEM((rows, amp_dev, depth), jnp.float32),
            pltpu.SemaphoreType.DMA((rows,)),
        ],
        compiler_params=limit(8 * rows * amp_dev * depth),
        cost_estimate=cost(0, 8 * rows * amp_dev * depth),
        name="load_amplitudes",
    )(in_hbm(amplitudes))


def coefficients(lists_ref, table_ref, amp_dev, lanes, blocks):
    lane = lax.axis_index("wide")
    grp = lax.axis_index("grp")
    amp, cint, res = (lists_ref[i] for i in range(3))
    local = amp - lane * amp_dev
    valid = (res >= 0) & (local >= 0) & (local < amp_dev)
    pos = jnp.zeros_like(res)
    for p in range(lanes):
        pos = jnp.where(res == table_ref[1:2, p : p + 1], p, pos)
    offset = pos ^ lane
    place = jnp.zeros_like(res)
    away, side = tile_order(lanes)
    for j, k in enumerate(away + side):
        place = jnp.where(offset == k, j, place)
    seg = jnp.where(valid, place * blocks + (cint ^ grp), -1)
    half = lanes // 2
    group = DEEP // (2 * amp_dev)
    rows = 2 * blocks * group * half
    slots = amp.shape[1]

    def parts(row):
        tile = row & (half - 1)
        inner = (row >> (half.bit_length() - 1)) & (group - 1)
        outer = row >> ((half * group).bit_length() - 1)
        return tile, inner, outer & (blocks - 1), outer >> (blocks.bit_length() - 1)

    tile, _, block, away_or_side = parts(lax.broadcasted_iota(jnp.int32, (rows, slots), 0))
    row_seg = (away_or_side * half + tile) * blocks + block
    col_amp = lax.broadcasted_iota(jnp.int32, (DEEP, slots), 0) & (amp_dev - 1)
    counts = jnp.zeros((rows, DEEP), jnp.float32)
    for src in range(lanes):
        hit_row = jnp.where(row_seg == seg[src : src + 1, :], 1.0, 0.0)
        hit_col = jnp.where(col_amp == local[src : src + 1, :], 1.0, 0.0)
        counts += lax.dot_general(
            hit_row.astype(jnp.bfloat16),
            hit_col.astype(jnp.bfloat16),
            (((1,), (1,)), ((), ())),
            preferred_element_type=jnp.float32,
        )
    _, inner, block, _ = parts(lax.broadcasted_iota(jnp.int32, (rows, DEEP), 0))
    block = block ^ grp
    label = jnp.zeros((rows, DEEP), jnp.int32)
    for c in range(blocks):
        label = jnp.where(block == c, table_ref[2:3, c : c + 1], label)
    odd = (label + table_ref[0:1, :]) & 1
    col = lax.broadcasted_iota(jnp.int32, (rows, DEEP), 1)
    same = inner == (col >> ((2 * amp_dev).bit_length() - 1))
    weight = jnp.where(odd == 1, -counts, counts)
    return jnp.where(same, weight, 0.0).astype(jnp.bfloat16)


def passes(hi, lo, in_hi, in_lo):
    dot = functools.partial(jnp.dot, preferred_element_type=jnp.float32)
    return dot(hi, in_hi) + dot(hi, in_lo) + dot(lo, in_hi)


def store_tiles(out, out_refs, held):
    tiles = len(out_refs)
    rows = out.shape[0] // tiles
    for b in range(held.shape[0]):
        held[b] = out[:, b * LANES : (b + 1) * LANES]
    for j, ref in enumerate(out_refs):
        for b in range(held.shape[0]):
            ref[0, :, b * LANES : (b + 1) * LANES] = held[b, pl.ds(j, rows, stride=tiles), :]


def sums_kernel(lanes, blocks, amp_dev, lists_ref, table_ref, own_ref, pair_ref, *refs):
    amp_refs, sums_refs, (local_ref, in_hi, in_lo) = refs[:2], refs[2:6], refs[6:]
    weight = coefficients(lists_ref, table_ref, amp_dev, lanes, blocks)
    depth = own_ref.shape[0]
    step = weight.shape[0] // (2 * blocks)
    first = 0
    for ref in amp_refs:
        count = ref.shape[0] // DEEP
        for g in range(count):
            rows = ref[g * DEEP : (g + 1) * DEEP, :]
            total = jnp.dot(weight, rows, preferred_element_type=jnp.float32)
            at = slice((first + g) * step, (first + g + 1) * step)
            for k in range(2):
                for c in range(blocks):
                    r = (k * blocks + c) * step
                    hi, lo = split(total[r : r + step, :])
                    sums_refs[2 * k][at, c * depth : (c + 1) * depth] = hi
                    sums_refs[2 * k + 1][at, c * depth : (c + 1) * depth] = lo
        first += count
    for c, ref in enumerate((own_ref, pair_ref)):
        hi, lo = split(ref[...])
        in_hi[c * depth : (c + 1) * depth, :] = hi
        in_lo[c * depth : (c + 1) * depth, :] = lo
    hi, lo = (x[:, : 2 * depth] for x in sums_refs[:2])
    local_ref[...] = passes(hi, lo, in_hi[...], in_lo[...])


def sums(lists, table, own, pair, rows, amp_dev, tile_rows, lanes, blocks):
    depth, window = own.shape
    kept = lanes // 2 * tile_rows
    held = pltpu.VMEM((kept, blocks * depth), jnp.bfloat16)
    local = pltpu.VMEM((2 * depth, window), jnp.bfloat16)
    product = pltpu.VMEM((kept, window), jnp.float32)
    return pl.pallas_call(
        functools.partial(sums_kernel, lanes, blocks, amp_dev),
        out_shape=[held] * 4 + [product] + [local] * 2,
        in_specs=[VMEM] * (4 + len(rows)),
        out_specs=[VMEM] * 7,
        compiler_params=limit(16 * depth * window),
        cost_estimate=cost(0, 16 * tile_rows * amp_dev * depth),
        name="sums",
    )(lists, table, own, pair, *[in_vmem(x) for x in rows])


def split_parts(parts, in_hi, in_lo):
    depth = sum(x.shape[0] for x in parts[:3])
    mine, theirs = end_offsets(depth)
    for c in range(len(parts) // 3):
        starts = (mine, row_cuts(depth)[0], theirs)
        for start, part in zip(starts, parts[3 * c : 3 * c + 3]):
            hi, lo = split(part[...])
            at = pl.ds(pl.multiple_of(c * depth + start, 16), part.shape[0])
            in_hi[at, :] = hi
            in_lo[at, :] = lo


def columns(x, odd, depth):
    blocks = range(2 + odd, x.shape[1] // depth, 2)
    return jnp.concatenate([x[:, c * depth : (c + 1) * depth] for c in blocks], axis=1)


def fetched_kernel(*refs):
    sums_refs, (local_ref, local_hi, local_lo), rest = refs[:4], refs[4:7], refs[7:]
    parts, out_refs, (in_hi, in_lo) = rest[:-4], rest[-4:-2], rest[-2:]
    depth = sum(x.shape[0] for x in parts[:3])
    split_parts(parts, in_hi, in_lo)
    hi, lo = (x[:, : 2 * depth] for x in sums_refs[2:])
    out_refs[1][...] = passes(hi, lo, local_hi[...], local_lo[...])
    for k, ref in enumerate((local_ref, out_refs[1])):
        hi, lo = (columns(x, 0, depth) for x in sums_refs[2 * k : 2 * k + 2])
        out_refs[k][...] = ref[...] + passes(hi, lo, in_hi[...], in_lo[...])


def flat(parts):
    return [x for three in parts for x in three]


def fetched_products(held, local, parts):
    rows, window = local[0].shape
    depth = sum(x.shape[0] for x in parts[0])
    half = pltpu.VMEM((len(parts) * depth, window), jnp.bfloat16)
    return pl.pallas_call(
        fetched_kernel,
        out_shape=[pltpu.VMEM((rows, window), jnp.float32)] * 2,
        in_specs=[VMEM] * (7 + 3 * len(parts)),
        out_specs=[VMEM] * 2,
        scratch_shapes=[half] * 2,
        compiler_params=limit(16 * len(parts) * depth * window),
        cost_estimate=cost(12 * rows * len(parts) * depth * window, 0),
        name="fetched_products",
    )(*[in_vmem(x) for x in (*held, *local)], *flat(parts))


def away_kernel(tiles, hi, lo, local_ref, *rest):
    parts, out_refs, (in_hi, in_lo, held) = rest[: -3 - tiles], rest[-3 - tiles : -3], rest[-3:]
    split_parts(parts, in_hi, in_lo)
    depth = sum(x.shape[0] for x in parts[:3])
    out = passes(columns(hi, 1, depth), columns(lo, 1, depth), in_hi[...], in_lo[...])
    store_tiles(local_ref[...] + out, out_refs, held)


def side_kernel(depth, hi, lo, local_ref, in_hi, in_lo, *rest):
    out_refs, held = rest[:-1], rest[-1]
    out = passes(columns(hi, 1, depth), columns(lo, 1, depth), in_hi[...], in_lo[...])
    store_tiles(local_ref[...] + out, out_refs, held)


def away_products(hi, lo, local, parts, tiles):
    rows, window = local.shape
    depth = sum(x.shape[0] for x in parts[0])
    remote = pltpu.VMEM((len(parts) * depth, window), jnp.bfloat16)
    shapes = [jax.ShapeDtypeStruct((1, rows // tiles, window), jnp.float32)] * tiles
    *out, in_hi, in_lo = pl.pallas_call(
        functools.partial(away_kernel, tiles),
        out_shape=shapes + [remote] * 2,
        in_specs=[VMEM] * (3 + 3 * len(parts)),
        out_specs=[VMEM] * (tiles + 2),
        scratch_shapes=[pltpu.VMEM((window // LANES, rows, LANES), jnp.float32)],
        compiler_params=limit(16 * len(parts) * depth * window),
        cost_estimate=cost(6 * rows * len(parts) * depth * window, 0),
        name="away_products",
    )(*[in_vmem(x) for x in (hi, lo, local)], *flat(parts))
    return out, in_hi, in_lo


def side_products(hi, lo, local, in_hi, in_lo, tiles, depth):
    rows, window = local.shape
    shapes = [jax.ShapeDtypeStruct((1, rows // tiles, window), jnp.float32)] * tiles
    return pl.pallas_call(
        functools.partial(side_kernel, depth),
        out_shape=shapes,
        in_specs=[VMEM] * 5,
        out_specs=[VMEM] * tiles,
        scratch_shapes=[pltpu.VMEM((window // LANES, rows, LANES), jnp.float32)],
        compiler_params=limit(0),
        cost_estimate=cost(0, 0),
        name="side_products",
    )(*[in_vmem(x) for x in (hi, lo, local, in_hi, in_lo)])


def on_device(
    amplitudes,
    integrals,
    base_residual,
    occ_gap,
    virt_sum,
    task_amp,
    task_int,
    task_res,
    task_count,
    res_owner,
    amp_label,
    int_label,
):
    lanes = lax.axis_size("wide")
    grps = lax.axis_size("grp")
    amp_dev, tile_rows, _ = amplitudes.shape
    half = lanes // 2
    own = integrals[0]
    one, two = pieces(own)
    fetched = {k: [swap(x, "grp", k) for x in (one, two)] for k in range(2, grps, 2)}
    lists, table = pack_lists(
        task_amp, task_int, after(task_res, one), task_count, amp_label, res_owner, int_label
    )
    pair = swap(own, "grp", 1)
    rows = [load(amplitudes, i * tile_rows // 2, tile_rows // 2) for i in range(2)]
    k = 1
    while k < lanes:
        if k == 2:
            lists = after(lists, rows[0])
        lists = jnp.concatenate([lists, swap(lists, "wide", k)], axis=1)
        k *= 2
    lists = after(lists, rows[1])
    *held, local_away, local_hi, local_lo = sums(
        lists, table, own, pair, rows, amp_dev, tile_rows, lanes, grps
    )

    even, odd = [], []
    for k, (one, two) in fetched.items():
        even.append([one, two, swap(one, "wide", 1)])
        odd.append([swap(after(x, y), "grp", 1) for x, y in zip(even[-1], (lists, held[0], held[0]))])

    local = fetched_products(held, (local_away, local_hi, local_lo), even)
    away, in_hi, in_lo = away_products(*held[:2], local[0], odd, half)
    _, offsets = tile_order(lanes)
    far, near, last = range(lanes // 4), range(lanes // 4, half - 1), half - 1
    side = side_products(*held[2:], local[1], in_hi, in_lo, half, own.shape[0])
    got = [swap(away[j], "wide", 1) for j in far]
    summed = base_residual + side[last]
    for j in far:
        summed = summed + swap(side[j] + got[j], "wide", offsets[j])
    rest = away[last]
    for j in near:
        summed = summed + swap(side[j], "wide", offsets[j])
        rest = rest + swap(after(away[j], side[0]), "wide", offsets[j])
    summed = summed + swap(rest, "wide", 1)
    divisor = occ_gap[:, :, None] + virt_sum[None, None, :]
    return summed / divisor


def solution(mesh):
    return jax.shard_map(
        on_device,
        mesh=mesh,
        in_specs=(
            P(("grp", "wide"), None, None),
            P("grp", None, None),
            P(("grp", "wide"), None, None),
            P(("grp", "wide"), None),
            P(),
            P(("grp", "wide"), None),
            P(("grp", "wide"), None),
            P(("grp", "wide"), None),
            P(("grp", "wide")),
            P("grp", None),
            P(("grp", "wide")),
            P(),
        ),
        out_specs=P(("grp", "wide"), None, None),
        check_vma=False,
    )
```

```python
import functools

import jax
import jax.numpy as jnp
from jax import lax
from jax.experimental import pallas as pl
from jax.experimental.pallas import tpu as pltpu
from jax.sharding import PartitionSpec as P

LANES = 128
MIB = 1024 * 1024
DEEP = 256
VMEM = pl.BlockSpec(memory_space=pltpu.VMEM)
HBM = pl.BlockSpec(memory_space=pltpu.HBM)


def in_vmem(x):
    return pltpu.with_memory_space_constraint(x, pltpu.VMEM)


def in_hbm(x):
    return pltpu.with_memory_space_constraint(x, pltpu.HBM)


def limit(n):
    return pltpu.CompilerParams(vmem_limit_bytes=min(n + 12 * MIB, 56 * MIB))


def cost(flops, nbytes):
    return pl.CostEstimate(flops=flops, bytes_accessed=nbytes, transcendentals=0)


def split(x):
    hi = x.astype(jnp.bfloat16)
    return hi, (x - hi.astype(jnp.float32)).astype(jnp.bfloat16)


def swap(x, axis, k):
    n = lax.axis_size(axis)
    return lax.ppermute(x, axis, [(i, i ^ k) for i in range(n)])


def after(x, *others):
    return lax.optimization_barrier((x, *others))[0]


def tile_order(lanes):
    half = lanes // 2
    side = list(range(half, lanes, 2)) + list(range(half - 2, -1, -2))
    return [k + 1 for k in side], side


def row_cuts(depth):
    end = depth * 9 // 32 // 16 * 16
    return end, depth - 2 * end


def end_offsets(depth):
    low = lax.axis_index("wide") & 1
    last = depth - row_cuts(depth)[0]
    return pl.multiple_of(low * last, 16), pl.multiple_of(last - low * last, 16)


def pieces_kernel(own_hbm, one_ref, two_ref, sems):
    end, middle = one_ref.shape[0], two_ref.shape[0]
    mine, _ = end_offsets(own_hbm.shape[0])
    copies = [
        pltpu.make_async_copy(own_hbm.at[pl.ds(mine, end), :], one_ref, sems.at[0]),
        pltpu.make_async_copy(own_hbm.at[pl.ds(end, middle), :], two_ref, sems.at[1]),
    ]
    for copy in copies:
        copy.start()
    for copy in copies:
        copy.wait()


def pieces(own):
    return pl.pallas_call(
        pieces_kernel,
        out_shape=[pltpu.VMEM((n, own.shape[1]), own.dtype) for n in row_cuts(own.shape[0])],
        in_specs=[HBM],
        out_specs=[VMEM] * 2,
        scratch_shapes=[pltpu.SemaphoreType.DMA((2,))],
        compiler_params=limit(0),
        cost_estimate=cost(0, own.size * 4),
        name="pieces",
    )(in_hbm(own))


def lists_kernel(count_ref, *refs):
    small, (lists_ref, table_ref) = refs[:6], refs[6:8]
    held, sems = refs[8:14], refs[14]
    amp, cint, res, amp_label, owner, int_label = held
    copies = [pltpu.make_async_copy(a, b, sems.at[i]) for i, (a, b) in enumerate(zip(small, held))]
    for copy in copies:
        copy.start()
    table_ref[...] = jnp.zeros(table_ref.shape, jnp.int32)
    for copy in copies:
        copy.wait()
    slot = lax.broadcasted_iota(jnp.int32, amp.shape, 1)
    lists_ref[0] = amp[...]
    lists_ref[1] = cint[...]
    lists_ref[2] = jnp.where(slot < count_ref[0], res[...], -1)
    amp_dev = amp_label.shape[1]
    for at in range(0, DEEP, amp_dev):
        table_ref[0:1, at : at + amp_dev] = amp_label[...]
    table_ref[1:2, 0 : owner.shape[1]] = owner[...]
    table_ref[2:3, 0 : int_label.shape[1]] = int_label[...]


def pack_lists(task_amp, task_int, task_res, task_count, amp_label, owner, int_label):
    args = [task_amp, task_int, task_res, amp_label[None, :], owner, int_label[None, :]]
    return pl.pallas_call(
        lists_kernel,
        out_shape=[
            pltpu.VMEM((3,) + task_amp.shape, jnp.int32),
            pltpu.VMEM((3, DEEP), jnp.int32),
        ],
        in_specs=[pl.BlockSpec(memory_space=pltpu.SMEM)] + [HBM] * 6,
        out_specs=[VMEM] * 2,
        scratch_shapes=[pltpu.VMEM(x.shape, x.dtype) for x in args]
        + [pltpu.SemaphoreType.DMA((6,))],
        compiler_params=limit(0),
        cost_estimate=cost(0, 4096),
        name="pack_lists",
    )(task_count, *[in_hbm(x) for x in args])


def load_kernel(first, amp_hbm, out_ref, rows_ref, sems):
    amp_dev = amp_hbm.shape[0]
    rows = rows_ref.shape[0]
    copies = [
        pltpu.make_async_copy(amp_hbm.at[:, first + i, :], rows_ref.at[i], sems.at[i])
        for i in range(rows)
    ]
    for copy in copies:
        copy.start()
    for i, copy in enumerate(copies):
        copy.wait()
        hi, lo = split(rows_ref[i])
        at = 2 * amp_dev * i
        out_ref[at : at + amp_dev, :] = hi
        out_ref[at + amp_dev : at + 2 * amp_dev, :] = lo


def load(amplitudes, first, rows):
    amp_dev, _, depth = amplitudes.shape
    return pl.pallas_call(
        functools.partial(load_kernel, first),
        out_shape=pltpu.VMEM((rows * 2 * amp_dev, depth), jnp.bfloat16),
        in_specs=[HBM],
        out_specs=VMEM,
        scratch_shapes=[
            pltpu.VMEM((rows, amp_dev, depth), jnp.float32),
            pltpu.SemaphoreType.DMA((rows,)),
        ],
        compiler_params=limit(8 * rows * amp_dev * depth),
        cost_estimate=cost(0, 8 * rows * amp_dev * depth),
        name="load_amplitudes",
    )(in_hbm(amplitudes))


def coefficients(lists_ref, table_ref, amp_dev, lanes, blocks):
    lane = lax.axis_index("wide")
    grp = lax.axis_index("grp")
    amp, cint, res = (lists_ref[i] for i in range(3))
    local = amp - lane * amp_dev
    valid = (res >= 0) & (local >= 0) & (local < amp_dev)
    pos = jnp.zeros_like(res)
    for p in range(lanes):
        pos = jnp.where(res == table_ref[1:2, p : p + 1], p, pos)
    offset = pos ^ lane
    place = jnp.zeros_like(res)
    away, side = tile_order(lanes)
    for j, k in enumerate(away + side):
        place = jnp.where(offset == k, j, place)
    seg = jnp.where(valid, place * blocks + (cint ^ grp), -1)
    half = lanes // 2
    group = DEEP // (2 * amp_dev)
    rows = 2 * blocks * group * half
    slots = amp.shape[1]

    def parts(row):
        tile = row & (half - 1)
        inner = (row >> (half.bit_length() - 1)) & (group - 1)
        outer = row >> ((half * group).bit_length() - 1)
        return tile, inner, outer & (blocks - 1), outer >> (blocks.bit_length() - 1)

    tile, _, block, away_or_side = parts(lax.broadcasted_iota(jnp.int32, (rows, slots), 0))
    row_seg = (away_or_side * half + tile) * blocks + block
    col_amp = lax.broadcasted_iota(jnp.int32, (DEEP, slots), 0) & (amp_dev - 1)
    counts = jnp.zeros((rows, DEEP), jnp.float32)
    for src in range(lanes):
        hit_row = jnp.where(row_seg == seg[src : src + 1, :], 1.0, 0.0)
        hit_col = jnp.where(col_amp == local[src : src + 1, :], 1.0, 0.0)
        counts += lax.dot_general(
            hit_row.astype(jnp.bfloat16),
            hit_col.astype(jnp.bfloat16),
            (((1,), (1,)), ((), ())),
            preferred_element_type=jnp.float32,
        )
    _, inner, block, _ = parts(lax.broadcasted_iota(jnp.int32, (rows, DEEP), 0))
    block = block ^ grp
    label = jnp.zeros((rows, DEEP), jnp.int32)
    for c in range(blocks):
        label = jnp.where(block == c, table_ref[2:3, c : c + 1], label)
    odd = (label + table_ref[0:1, :]) & 1
    col = lax.broadcasted_iota(jnp.int32, (rows, DEEP), 1)
    same = inner == (col >> ((2 * amp_dev).bit_length() - 1))
    weight = jnp.where(odd == 1, -counts, counts)
    return jnp.where(same, weight, 0.0).astype(jnp.bfloat16)


def passes(hi, lo, in_hi, in_lo):
    dot = functools.partial(jnp.dot, preferred_element_type=jnp.float32)
    return dot(hi, in_hi) + dot(hi, in_lo) + dot(lo, in_hi)


def store_tiles(out, out_refs, held):
    tiles = len(out_refs)
    rows = out.shape[0] // tiles
    for b in range(held.shape[0]):
        held[b] = out[:, b * LANES : (b + 1) * LANES]
    for j, ref in enumerate(out_refs):
        for b in range(held.shape[0]):
            ref[0, :, b * LANES : (b + 1) * LANES] = held[b, pl.ds(j, rows, stride=tiles), :]


def sums_kernel(lanes, blocks, amp_dev, lists_ref, table_ref, own_ref, pair_ref, *refs):
    amp_refs, sums_refs, local_refs, (in_hi, in_lo) = refs[:2], refs[2:6], refs[6:8], refs[8:]
    weight = coefficients(lists_ref, table_ref, amp_dev, lanes, blocks)
    depth = own_ref.shape[0]
    step = weight.shape[0] // (2 * blocks)
    first = 0
    for ref in amp_refs:
        count = ref.shape[0] // DEEP
        for g in range(count):
            rows = ref[g * DEEP : (g + 1) * DEEP, :]
            total = jnp.dot(weight, rows, preferred_element_type=jnp.float32)
            at = slice((first + g) * step, (first + g + 1) * step)
            for k in range(2):
                for c in range(blocks):
                    r = (k * blocks + c) * step
                    hi, lo = split(total[r : r + step, :])
                    sums_refs[2 * k][at, c * depth : (c + 1) * depth] = hi
                    sums_refs[2 * k + 1][at, c * depth : (c + 1) * depth] = lo
        first += count
    for c, ref in enumerate((own_ref, pair_ref)):
        hi, lo = split(ref[...])
        in_hi[c * depth : (c + 1) * depth, :] = hi
        in_lo[c * depth : (c + 1) * depth, :] = lo
    for k, ref in enumerate(local_refs):
        hi, lo = (x[:, : 2 * depth] for x in sums_refs[2 * k : 2 * k + 2])
        ref[...] = passes(hi, lo, in_hi[...], in_lo[...])


def sums(lists, table, own, pair, rows, amp_dev, tile_rows, lanes, blocks):
    depth, window = own.shape
    kept = lanes // 2 * tile_rows
    held = pltpu.VMEM((kept, blocks * depth), jnp.bfloat16)
    local = pltpu.VMEM((2 * depth, window), jnp.bfloat16)
    product = pltpu.VMEM((kept, window), jnp.float32)
    return pl.pallas_call(
        functools.partial(sums_kernel, lanes, blocks, amp_dev),
        out_shape=[held] * 4 + [product] * 2,
        in_specs=[VMEM] * (4 + len(rows)),
        out_specs=[VMEM] * 6,
        scratch_shapes=[local] * 2,
        compiler_params=limit(16 * depth * window),
        cost_estimate=cost(0, 16 * tile_rows * amp_dev * depth),
        name="sums",
    )(lists, table, own, pair, *[in_vmem(x) for x in rows])


def split_parts(parts, in_hi, in_lo, cuts):
    n = sum(cuts)
    depth = in_hi.shape[0] // (len(parts) // n)
    mine, theirs = end_offsets(depth)
    end, middle = row_cuts(depth)
    places = zip((mine, end, theirs), (end, middle, end), cuts)
    starts = [first + i * rows // m for first, rows, m in places for i in range(m)]
    for i, part in enumerate(parts):
        hi, lo = split(part[...])
        at = pl.ds(pl.multiple_of(i // n * depth + starts[i % n], 16), part.shape[0])
        in_hi[at, :] = hi
        in_lo[at, :] = lo


def columns(x, odd, depth):
    blocks = range(2 + odd, x.shape[1] // depth, 2)
    return jnp.concatenate([x[:, c * depth : (c + 1) * depth] for c in blocks], axis=1)


def fetched_kernel(*refs):
    sums_refs, local_refs, rest = refs[:4], refs[4:6], refs[6:]
    parts, out_refs, (in_hi, in_lo) = rest[:-4], rest[-4:-2], rest[-2:]
    depth = sum(x.shape[0] for x in parts[:3])
    split_parts(parts, in_hi, in_lo, (1, 1, 1))
    for k in range(2):
        hi, lo = (columns(x, 0, depth) for x in sums_refs[2 * k : 2 * k + 2])
        out_refs[k][...] = local_refs[k][...] + passes(hi, lo, in_hi[...], in_lo[...])


def flat(parts):
    return [x for three in parts for x in three]


def fetched_products(held, local, parts):
    rows, window = local[0].shape
    depth = sum(x.shape[0] for x in parts[0])
    half = pltpu.VMEM((len(parts) * depth, window), jnp.bfloat16)
    return pl.pallas_call(
        fetched_kernel,
        out_shape=[pltpu.VMEM((rows, window), jnp.float32)] * 2,
        in_specs=[VMEM] * (6 + 3 * len(parts)),
        out_specs=[VMEM] * 2,
        scratch_shapes=[half] * 2,
        compiler_params=limit(16 * len(parts) * depth * window),
        cost_estimate=cost(12 * rows * len(parts) * depth * window, 0),
        name="fetched_products",
    )(*[in_vmem(x) for x in (*held, *local)], *flat(parts))


def away_kernel(tiles, hi, lo, local_ref, *rest):
    parts, out_refs, (in_hi, in_lo, held) = rest[: -3 - tiles], rest[-3 - tiles : -3], rest[-3:]
    split_parts(parts, in_hi, in_lo, (1, 2, 2))
    depth = in_hi.shape[0] // (len(parts) // 5)
    out = passes(columns(hi, 1, depth), columns(lo, 1, depth), in_hi[...], in_lo[...])
    store_tiles(local_ref[...] + out, out_refs, held)


def side_kernel(depth, hi, lo, local_ref, in_hi, in_lo, *rest):
    out_refs, held = rest[:-1], rest[-1]
    out = passes(columns(hi, 1, depth), columns(lo, 1, depth), in_hi[...], in_lo[...])
    store_tiles(local_ref[...] + out, out_refs, held)


def away_products(hi, lo, local, parts, tiles):
    rows, window = local.shape
    depth = sum(x.shape[0] for x in parts[0])
    remote = pltpu.VMEM((len(parts) * depth, window), jnp.bfloat16)
    shapes = [jax.ShapeDtypeStruct((1, rows // tiles, window), jnp.float32)] * tiles
    *out, in_hi, in_lo = pl.pallas_call(
        functools.partial(away_kernel, tiles),
        out_shape=shapes + [remote] * 2,
        in_specs=[VMEM] * (3 + 5 * len(parts)),
        out_specs=[VMEM] * (tiles + 2),
        scratch_shapes=[pltpu.VMEM((window // LANES, rows, LANES), jnp.float32)],
        compiler_params=limit(16 * len(parts) * depth * window),
        cost_estimate=cost(6 * rows * len(parts) * depth * window, 0),
        name="away_products",
    )(*[in_vmem(x) for x in (hi, lo, local)], *flat(parts))
    return out, in_hi, in_lo


def side_products(hi, lo, local, in_hi, in_lo, tiles, depth):
    rows, window = local.shape
    shapes = [jax.ShapeDtypeStruct((1, rows // tiles, window), jnp.float32)] * tiles
    return pl.pallas_call(
        functools.partial(side_kernel, depth),
        out_shape=shapes,
        in_specs=[VMEM] * 5,
        out_specs=[VMEM] * tiles,
        scratch_shapes=[pltpu.VMEM((window // LANES, rows, LANES), jnp.float32)],
        compiler_params=limit(0),
        cost_estimate=cost(0, 0),
        name="side_products",
    )(*[in_vmem(x) for x in (hi, lo, local, in_hi, in_lo)])


def halves_kernel(x, *out_refs):
    rows = out_refs[0].shape[0]
    for i, ref in enumerate(out_refs):
        ref[...] = x[i * rows : (i + 1) * rows, :]


def halves(x, nbytes):
    half = pltpu.VMEM((x.shape[0] // 2, x.shape[1]), x.dtype)
    return pl.pallas_call(
        halves_kernel,
        out_shape=[half, half],
        in_specs=[VMEM],
        out_specs=[VMEM] * 2,
        compiler_params=limit(0),
        cost_estimate=cost(0, nbytes),
        name="halves",
    )(x)


def on_device(
    amplitudes,
    integrals,
    base_residual,
    occ_gap,
    virt_sum,
    task_amp,
    task_int,
    task_res,
    task_count,
    res_owner,
    amp_label,
    int_label,
):
    lanes = lax.axis_size("wide")
    grps = lax.axis_size("grp")
    amp_dev, tile_rows, _ = amplitudes.shape
    half = lanes // 2
    own = integrals[0]
    one, two = pieces(own)
    fetched = {k: [swap(x, "grp", k) for x in (one, two)] for k in range(2, grps, 2)}
    lists, table = pack_lists(
        task_amp, task_int, after(task_res, one), task_count, amp_label, res_owner, int_label
    )
    pair = swap(own, "grp", 1)
    rows = [load(amplitudes, i * tile_rows // 2, tile_rows // 2) for i in range(2)]
    k = 1
    while k < lanes:
        if k == 2:
            lists = after(lists, rows[0])
        lists = jnp.concatenate([lists, swap(lists, "wide", k)], axis=1)
        k *= 2
    lists = after(lists, rows[1])
    *held, local_away, local_side = sums(
        lists, table, own, pair, rows, amp_dev, tile_rows, lanes, grps
    )

    even, odd = [], []
    for k, (one, two) in fetched.items():
        even.append([one, two, swap(one, "wide", 1)])
        later = [one, *halves(after(two, held[0]), 0), *halves(after(even[-1][2], held[0]), 0)]
        odd.append([swap(after(x, held[0]), "grp", 1) for x in later])

    local = fetched_products(held, (local_away, local_side), even)
    away, in_hi, in_lo = away_products(*held[:2], local[0], odd, half)
    _, offsets = tile_order(lanes)
    far, near, last = range(lanes // 4), range(lanes // 4, half - 1), half - 1
    side = side_products(*held[2:], local[1], in_hi, in_lo, half, own.shape[0])
    got = [swap(away[j], "wide", 1) for j in far]
    summed = base_residual + side[last]
    for j in far:
        summed = summed + swap(side[j] + got[j], "wide", offsets[j])
    rest = away[last]
    for j in near:
        summed = summed + swap(side[j], "wide", offsets[j])
        rest = rest + swap(after(away[j], side[0]), "wide", offsets[j])
    summed = summed + swap(rest, "wide", 1)
    divisor = occ_gap[:, :, None] + virt_sum[None, None, :]
    return summed / divisor


def solution(mesh):
    return jax.shard_map(
        on_device,
        mesh=mesh,
        in_specs=(
            P(("grp", "wide"), None, None),
            P("grp", None, None),
            P(("grp", "wide"), None, None),
            P(("grp", "wide"), None),
            P(),
            P(("grp", "wide"), None),
            P(("grp", "wide"), None),
            P(("grp", "wide"), None),
            P(("grp", "wide")),
            P("grp", None),
            P(("grp", "wide")),
            P(),
        ),
        out_specs=P(("grp", "wide"), None, None),
        check_vma=False,
    )
```

```python
import functools

import jax
import jax.numpy as jnp
from jax import lax
from jax.experimental import pallas as pl
from jax.experimental.pallas import tpu as pltpu
from jax.sharding import PartitionSpec as P

LANES = 128
MIB = 1024 * 1024
DEEP = 256
VMEM = pl.BlockSpec(memory_space=pltpu.VMEM)
HBM = pl.BlockSpec(memory_space=pltpu.HBM)


def in_vmem(x):
    return pltpu.with_memory_space_constraint(x, pltpu.VMEM)


def in_hbm(x):
    return pltpu.with_memory_space_constraint(x, pltpu.HBM)


def limit(n):
    return pltpu.CompilerParams(vmem_limit_bytes=min(n + 12 * MIB, 56 * MIB))


def cost(flops, nbytes):
    return pl.CostEstimate(flops=flops, bytes_accessed=nbytes, transcendentals=0)


def split(x):
    hi = x.astype(jnp.bfloat16)
    return hi, (x - hi.astype(jnp.float32)).astype(jnp.bfloat16)


def swap(x, axis, k):
    n = lax.axis_size(axis)
    return lax.ppermute(x, axis, [(i, i ^ k) for i in range(n)])


def after(x, *others):
    return lax.optimization_barrier((x, *others))[0]


def tile_order(lanes):
    half = lanes // 2
    side = list(range(half, lanes, 2)) + list(range(half - 2, -1, -2))
    return [k + 1 for k in side], side


def row_cuts(depth):
    end = depth * 9 // 32 // 16 * 16
    return end, depth - 2 * end


def end_offsets(depth):
    low = lax.axis_index("wide") & 1
    last = depth - row_cuts(depth)[0]
    return pl.multiple_of(low * last, 16), pl.multiple_of(last - low * last, 16)


def pieces_kernel(own_hbm, one_ref, two_ref, sems):
    end, middle = one_ref.shape[0], two_ref.shape[0]
    mine, _ = end_offsets(own_hbm.shape[0])
    copies = [
        pltpu.make_async_copy(own_hbm.at[pl.ds(mine, end), :], one_ref, sems.at[0]),
        pltpu.make_async_copy(own_hbm.at[pl.ds(end, middle), :], two_ref, sems.at[1]),
    ]
    for copy in copies:
        copy.start()
    for copy in copies:
        copy.wait()


def pieces(own):
    return pl.pallas_call(
        pieces_kernel,
        out_shape=[pltpu.VMEM((n, own.shape[1]), own.dtype) for n in row_cuts(own.shape[0])],
        in_specs=[HBM],
        out_specs=[VMEM] * 2,
        scratch_shapes=[pltpu.SemaphoreType.DMA((2,))],
        compiler_params=limit(0),
        cost_estimate=cost(0, own.size * 4),
        name="pieces",
    )(in_hbm(own))


def lists_kernel(count_ref, *refs):
    small, (lists_ref, table_ref) = refs[:6], refs[6:8]
    held, sems = refs[8:14], refs[14]
    amp, cint, res, amp_label, owner, int_label = held
    copies = [pltpu.make_async_copy(a, b, sems.at[i]) for i, (a, b) in enumerate(zip(small, held))]
    for copy in copies:
        copy.start()
    table_ref[...] = jnp.zeros(table_ref.shape, jnp.int32)
    for copy in copies:
        copy.wait()
    slot = lax.broadcasted_iota(jnp.int32, amp.shape, 1)
    lists_ref[0] = amp[...]
    lists_ref[1] = cint[...]
    lists_ref[2] = jnp.where(slot < count_ref[0], res[...], -1)
    amp_dev = amp_label.shape[1]
    for at in range(0, DEEP, amp_dev):
        table_ref[0:1, at : at + amp_dev] = amp_label[...]
    table_ref[1:2, 0 : owner.shape[1]] = owner[...]
    table_ref[2:3, 0 : int_label.shape[1]] = int_label[...]


def pack_lists(task_amp, task_int, task_res, task_count, amp_label, owner, int_label):
    args = [task_amp, task_int, task_res, amp_label[None, :], owner, int_label[None, :]]
    return pl.pallas_call(
        lists_kernel,
        out_shape=[
            pltpu.VMEM((3,) + task_amp.shape, jnp.int32),
            pltpu.VMEM((3, DEEP), jnp.int32),
        ],
        in_specs=[pl.BlockSpec(memory_space=pltpu.SMEM)] + [HBM] * 6,
        out_specs=[VMEM] * 2,
        scratch_shapes=[pltpu.VMEM(x.shape, x.dtype) for x in args]
        + [pltpu.SemaphoreType.DMA((6,))],
        compiler_params=limit(0),
        cost_estimate=cost(0, 4096),
        name="pack_lists",
    )(task_count, *[in_hbm(x) for x in args])


def load_kernel(first, amp_hbm, out_ref, rows_ref, sems):
    amp_dev = amp_hbm.shape[0]
    rows = rows_ref.shape[0]
    copies = [
        pltpu.make_async_copy(amp_hbm.at[:, first + i, :], rows_ref.at[i], sems.at[i])
        for i in range(rows)
    ]
    for copy in copies:
        copy.start()
    for i, copy in enumerate(copies):
        copy.wait()
        hi, lo = split(rows_ref[i])
        at = 2 * amp_dev * i
        out_ref[at : at + amp_dev, :] = hi
        out_ref[at + amp_dev : at + 2 * amp_dev, :] = lo


def load(amplitudes, first, rows):
    amp_dev, _, depth = amplitudes.shape
    return pl.pallas_call(
        functools.partial(load_kernel, first),
        out_shape=pltpu.VMEM((rows * 2 * amp_dev, depth), jnp.bfloat16),
        in_specs=[HBM],
        out_specs=VMEM,
        scratch_shapes=[
            pltpu.VMEM((rows, amp_dev, depth), jnp.float32),
            pltpu.SemaphoreType.DMA((rows,)),
        ],
        compiler_params=limit(8 * rows * amp_dev * depth),
        cost_estimate=cost(0, 8 * rows * amp_dev * depth),
        name="load_amplitudes",
    )(in_hbm(amplitudes))


def coefficients(lists_ref, table_ref, amp_dev, lanes, blocks):
    lane = lax.axis_index("wide")
    grp = lax.axis_index("grp")
    amp, cint, res = (lists_ref[i] for i in range(3))
    local = amp - lane * amp_dev
    valid = (res >= 0) & (local >= 0) & (local < amp_dev)
    pos = jnp.zeros_like(res)
    for p in range(lanes):
        pos = jnp.where(res == table_ref[1:2, p : p + 1], p, pos)
    offset = pos ^ lane
    place = jnp.zeros_like(res)
    away, side = tile_order(lanes)
    for j, k in enumerate(away + side):
        place = jnp.where(offset == k, j, place)
    seg = jnp.where(valid, place * blocks + (cint ^ grp), -1)
    half = lanes // 2
    group = DEEP // (2 * amp_dev)
    rows = 2 * blocks * group * half
    slots = amp.shape[1]

    def parts(row):
        tile = row & (half - 1)
        inner = (row >> (half.bit_length() - 1)) & (group - 1)
        outer = row >> ((half * group).bit_length() - 1)
        return tile, inner, outer & (blocks - 1), outer >> (blocks.bit_length() - 1)

    tile, _, block, away_or_side = parts(lax.broadcasted_iota(jnp.int32, (rows, slots), 0))
    row_seg = (away_or_side * half + tile) * blocks + block
    col_amp = lax.broadcasted_iota(jnp.int32, (DEEP, slots), 0) & (amp_dev - 1)
    counts = jnp.zeros((rows, DEEP), jnp.float32)
    for src in range(lanes):
        hit_row = jnp.where(row_seg == seg[src : src + 1, :], 1.0, 0.0)
        hit_col = jnp.where(col_amp == local[src : src + 1, :], 1.0, 0.0)
        counts += lax.dot_general(
            hit_row.astype(jnp.bfloat16),
            hit_col.astype(jnp.bfloat16),
            (((1,), (1,)), ((), ())),
            preferred_element_type=jnp.float32,
        )
    _, inner, block, _ = parts(lax.broadcasted_iota(jnp.int32, (rows, DEEP), 0))
    block = block ^ grp
    label = jnp.zeros((rows, DEEP), jnp.int32)
    for c in range(blocks):
        label = jnp.where(block == c, table_ref[2:3, c : c + 1], label)
    odd = (label + table_ref[0:1, :]) & 1
    col = lax.broadcasted_iota(jnp.int32, (rows, DEEP), 1)
    same = inner == (col >> ((2 * amp_dev).bit_length() - 1))
    weight = jnp.where(odd == 1, -counts, counts)
    return jnp.where(same, weight, 0.0).astype(jnp.bfloat16)


def passes(hi, lo, in_hi, in_lo):
    dot = functools.partial(jnp.dot, preferred_element_type=jnp.float32)
    return dot(hi, in_hi) + dot(hi, in_lo) + dot(lo, in_hi)


def store_tiles(out, out_refs, held):
    tiles = len(out_refs)
    rows = out.shape[0] // tiles
    for b in range(held.shape[0]):
        held[b] = out[:, b * LANES : (b + 1) * LANES]
    for j, ref in enumerate(out_refs):
        for b in range(held.shape[0]):
            ref[0, :, b * LANES : (b + 1) * LANES] = held[b, pl.ds(j, rows, stride=tiles), :]


def sums_kernel(lanes, blocks, amp_dev, lists_ref, table_ref, own_ref, pair_ref, *refs):
    amp_refs, sums_refs, (local_ref, in_hi, in_lo) = refs[:2], refs[2:6], refs[6:]
    weight = coefficients(lists_ref, table_ref, amp_dev, lanes, blocks)
    depth = own_ref.shape[0]
    step = weight.shape[0] // (2 * blocks)
    first = 0
    for ref in amp_refs:
        count = ref.shape[0] // DEEP
        for g in range(count):
            rows = ref[g * DEEP : (g + 1) * DEEP, :]
            total = jnp.dot(weight, rows, preferred_element_type=jnp.float32)
            at = slice((first + g) * step, (first + g + 1) * step)
            for k in range(2):
                for c in range(blocks):
                    r = (k * blocks + c) * step
                    hi, lo = split(total[r : r + step, :])
                    sums_refs[2 * k][at, c * depth : (c + 1) * depth] = hi
                    sums_refs[2 * k + 1][at, c * depth : (c + 1) * depth] = lo
        first += count
    for c, ref in enumerate((own_ref, pair_ref)):
        hi, lo = split(ref[...])
        in_hi[c * depth : (c + 1) * depth, :] = hi
        in_lo[c * depth : (c + 1) * depth, :] = lo
    hi, lo = (x[:, : 2 * depth] for x in sums_refs[:2])
    local_ref[...] = passes(hi, lo, in_hi[...], in_lo[...])


def sums(lists, table, own, pair, rows, amp_dev, tile_rows, lanes, blocks):
    depth, window = own.shape
    kept = lanes // 2 * tile_rows
    held = pltpu.VMEM((kept, blocks * depth), jnp.bfloat16)
    local = pltpu.VMEM((2 * depth, window), jnp.bfloat16)
    product = pltpu.VMEM((kept, window), jnp.float32)
    return pl.pallas_call(
        functools.partial(sums_kernel, lanes, blocks, amp_dev),
        out_shape=[held] * 4 + [product] + [local] * 2,
        in_specs=[VMEM] * (4 + len(rows)),
        out_specs=[VMEM] * 7,
        compiler_params=limit(16 * depth * window),
        cost_estimate=cost(0, 16 * tile_rows * amp_dev * depth),
        name="sums",
    )(lists, table, own, pair, *[in_vmem(x) for x in rows])


def split_parts(parts, in_hi, in_lo):
    depth = sum(x.shape[0] for x in parts[:3])
    mine, theirs = end_offsets(depth)
    for c in range(len(parts) // 3):
        starts = (mine, row_cuts(depth)[0], theirs)
        for start, part in zip(starts, parts[3 * c : 3 * c + 3]):
            hi, lo = split(part[...])
            at = pl.ds(pl.multiple_of(c * depth + start, 16), part.shape[0])
            in_hi[at, :] = hi
            in_lo[at, :] = lo


def columns(x, odd, depth):
    blocks = range(2 + odd, x.shape[1] // depth, 2)
    return jnp.concatenate([x[:, c * depth : (c + 1) * depth] for c in blocks], axis=1)


def fetched_kernel(*refs):
    sums_refs, (local_ref, local_hi, local_lo), rest = refs[:4], refs[4:7], refs[7:]
    parts, out_refs, (in_hi, in_lo) = rest[:-4], rest[-4:-2], rest[-2:]
    depth = sum(x.shape[0] for x in parts[:3])
    split_parts(parts, in_hi, in_lo)
    hi, lo = (x[:, : 2 * depth] for x in sums_refs[2:])
    out_refs[1][...] = passes(hi, lo, local_hi[...], local_lo[...])
    for k, ref in enumerate((local_ref, out_refs[1])):
        hi, lo = (columns(x, 0, depth) for x in sums_refs[2 * k : 2 * k + 2])
        out_refs[k][...] = ref[...] + passes(hi, lo, in_hi[...], in_lo[...])


def flat(parts):
    return [x for three in parts for x in three]


def fetched_products(held, local, parts):
    rows, window = local[0].shape
    depth = sum(x.shape[0] for x in parts[0])
    half = pltpu.VMEM((len(parts) * depth, window), jnp.bfloat16)
    return pl.pallas_call(
        fetched_kernel,
        out_shape=[pltpu.VMEM((rows, window), jnp.float32)] * 2,
        in_specs=[VMEM] * (7 + 3 * len(parts)),
        out_specs=[VMEM] * 2,
        scratch_shapes=[half] * 2,
        compiler_params=limit(16 * len(parts) * depth * window),
        cost_estimate=cost(12 * rows * len(parts) * depth * window, 0),
        name="fetched_products",
    )(*[in_vmem(x) for x in (*held, *local)], *flat(parts))


def away_kernel(tiles, hi, lo, local_ref, *rest):
    parts, out_refs, (in_hi, in_lo, held) = rest[: -3 - tiles], rest[-3 - tiles : -3], rest[-3:]
    split_parts(parts, in_hi, in_lo)
    depth = sum(x.shape[0] for x in parts[:3])
    out = passes(columns(hi, 1, depth), columns(lo, 1, depth), in_hi[...], in_lo[...])
    store_tiles(local_ref[...] + out, out_refs, held)


def side_kernel(depth, hi, lo, local_ref, in_hi, in_lo, *rest):
    out_refs, held = rest[:-1], rest[-1]
    out = passes(columns(hi, 1, depth), columns(lo, 1, depth), in_hi[...], in_lo[...])
    store_tiles(local_ref[...] + out, out_refs, held)


def away_products(hi, lo, local, parts, tiles):
    rows, window = local.shape
    depth = sum(x.shape[0] for x in parts[0])
    remote = pltpu.VMEM((len(parts) * depth, window), jnp.bfloat16)
    shapes = [jax.ShapeDtypeStruct((1, rows // tiles, window), jnp.float32)] * tiles
    *out, in_hi, in_lo = pl.pallas_call(
        functools.partial(away_kernel, tiles),
        out_shape=shapes + [remote] * 2,
        in_specs=[VMEM] * (3 + 3 * len(parts)),
        out_specs=[VMEM] * (tiles + 2),
        scratch_shapes=[pltpu.VMEM((window // LANES, rows, LANES), jnp.float32)],
        compiler_params=limit(16 * len(parts) * depth * window),
        cost_estimate=cost(6 * rows * len(parts) * depth * window, 0),
        name="away_products",
    )(*[in_vmem(x) for x in (hi, lo, local)], *flat(parts))
    return out, in_hi, in_lo


def side_products(hi, lo, local, in_hi, in_lo, tiles, depth):
    rows, window = local.shape
    shapes = [jax.ShapeDtypeStruct((1, rows // tiles, window), jnp.float32)] * tiles
    return pl.pallas_call(
        functools.partial(side_kernel, depth),
        out_shape=shapes,
        in_specs=[VMEM] * 5,
        out_specs=[VMEM] * tiles,
        scratch_shapes=[pltpu.VMEM((window // LANES, rows, LANES), jnp.float32)],
        compiler_params=limit(0),
        cost_estimate=cost(0, 0),
        name="side_products",
    )(*[in_vmem(x) for x in (hi, lo, local, in_hi, in_lo)])


def on_device(
    amplitudes,
    integrals,
    base_residual,
    occ_gap,
    virt_sum,
    task_amp,
    task_int,
    task_res,
    task_count,
    res_owner,
    amp_label,
    int_label,
):
    lanes = lax.axis_size("wide")
    grps = lax.axis_size("grp")
    amp_dev, tile_rows, _ = amplitudes.shape
    half = lanes // 2
    own = integrals[0]
    one, two = pieces(own)
    fetched = {k: [swap(x, "grp", k) for x in (one, two)] for k in range(2, grps, 2)}
    lists, table = pack_lists(
        task_amp, task_int, after(task_res, one), task_count, amp_label, res_owner, int_label
    )
    pair = swap(own, "grp", 1)
    rows = [load(amplitudes, i * tile_rows // 2, tile_rows // 2) for i in range(2)]
    order = [1] + [1 << b for b in range(lanes.bit_length() - 2, 0, -1)]
    for k in order:
        if k == order[1]:
            lists = after(lists, rows[0])
        lists = jnp.concatenate([lists, swap(lists, "wide", k)], axis=1)
    lists = after(lists, rows[1])
    *held, local_away, local_hi, local_lo = sums(
        lists, table, own, pair, rows, amp_dev, tile_rows, lanes, grps
    )

    even, odd = [], []
    for k, (one, two) in fetched.items():
        even.append([one, two, swap(one, "wide", 1)])
        odd.append([swap(after(x, y), "grp", 1) for x, y in zip(even[-1], (lists, held[0], held[0]))])

    local = fetched_products(held, (local_away, local_hi, local_lo), even)
    away, in_hi, in_lo = away_products(*held[:2], local[0], odd, half)
    _, offsets = tile_order(lanes)
    far, near, last = range(lanes // 4), range(lanes // 4, half - 1), half - 1
    side = side_products(*held[2:], local[1], in_hi, in_lo, half, own.shape[0])
    got = [swap(after(away[j], side[0]) if j else away[j], "wide", 1) for j in far]
    summed = base_residual + side[last]
    for j in far:
        summed = summed + swap(side[j] + got[j], "wide", offsets[j])
    rest = away[last]
    for j in near:
        summed = summed + swap(side[j], "wide", offsets[j])
        rest = rest + swap(away[j], "wide", offsets[j])
    summed = summed + swap(rest, "wide", 1)
    divisor = occ_gap[:, :, None] + virt_sum[None, None, :]
    return summed / divisor


def solution(mesh):
    return jax.shard_map(
        on_device,
        mesh=mesh,
        in_specs=(
            P(("grp", "wide"), None, None),
            P("grp", None, None),
            P(("grp", "wide"), None, None),
            P(("grp", "wide"), None),
            P(),
            P(("grp", "wide"), None),
            P(("grp", "wide"), None),
            P(("grp", "wide"), None),
            P(("grp", "wide")),
            P("grp", None),
            P(("grp", "wide")),
            P(),
        ),
        out_specs=P(("grp", "wide"), None, None),
        check_vma=False,
    )
```

```python
import functools

import jax
import jax.numpy as jnp
from jax import lax
from jax.experimental import pallas as pl
from jax.experimental.pallas import tpu as pltpu
from jax.sharding import PartitionSpec as P

LANES = 128
MIB = 1024 * 1024
DEEP = 256
VMEM = pl.BlockSpec(memory_space=pltpu.VMEM)
HBM = pl.BlockSpec(memory_space=pltpu.HBM)


def in_vmem(x):
    return pltpu.with_memory_space_constraint(x, pltpu.VMEM)


def in_hbm(x):
    return pltpu.with_memory_space_constraint(x, pltpu.HBM)


def limit(n):
    return pltpu.CompilerParams(vmem_limit_bytes=min(n + 12 * MIB, 56 * MIB))


def cost(flops, nbytes):
    return pl.CostEstimate(flops=flops, bytes_accessed=nbytes, transcendentals=0)


def split(x):
    hi = x.astype(jnp.bfloat16)
    return hi, (x - hi.astype(jnp.float32)).astype(jnp.bfloat16)


def swap(x, axis, k):
    n = lax.axis_size(axis)
    return lax.ppermute(x, axis, [(i, i ^ k) for i in range(n)])


def after(x, *others):
    return lax.optimization_barrier((x, *others))[0]


def tile_order(lanes):
    half = lanes // 2
    side = list(range(half, lanes, 2)) + list(range(half - 2, -1, -2))
    return [k + 1 for k in side], side


def row_cuts(depth):
    end = depth * 9 // 32 // 16 * 16
    return end, depth - 2 * end


def end_offsets(depth):
    low = lax.axis_index("wide") & 1
    last = depth - row_cuts(depth)[0]
    return pl.multiple_of(low * last, 16), pl.multiple_of(last - low * last, 16)


def piece_kernel(ends, own_hbm, out_ref, sem):
    rows = out_ref.shape[0]
    start = end_offsets(own_hbm.shape[0])[0] if ends else (own_hbm.shape[0] - rows) // 2
    copy = pltpu.make_async_copy(own_hbm.at[pl.ds(start, rows), :], out_ref, sem)
    copy.start()
    copy.wait()


def piece(own, ends):
    rows = row_cuts(own.shape[0])[0 if ends else 1]
    return pl.pallas_call(
        functools.partial(piece_kernel, ends),
        out_shape=pltpu.VMEM((rows, own.shape[1]), own.dtype),
        in_specs=[HBM],
        out_specs=VMEM,
        scratch_shapes=[pltpu.SemaphoreType.DMA],
        compiler_params=limit(0),
        cost_estimate=cost(0, own.size * 4),
        name="piece",
    )(in_hbm(own))


def lists_kernel(count_ref, *refs):
    small, (lists_ref, table_ref) = refs[:6], refs[6:8]
    held, sems = refs[8:14], refs[14]
    amp, cint, res, amp_label, owner, int_label = held
    copies = [pltpu.make_async_copy(a, b, sems.at[i]) for i, (a, b) in enumerate(zip(small, held))]
    for copy in copies:
        copy.start()
    table_ref[...] = jnp.zeros(table_ref.shape, jnp.int32)
    for copy in copies:
        copy.wait()
    slot = lax.broadcasted_iota(jnp.int32, amp.shape, 1)
    lists_ref[0] = amp[...]
    lists_ref[1] = cint[...]
    lists_ref[2] = jnp.where(slot < count_ref[0], res[...], -1)
    amp_dev = amp_label.shape[1]
    for at in range(0, DEEP, amp_dev):
        table_ref[0:1, at : at + amp_dev] = amp_label[...]
    table_ref[1:2, 0 : owner.shape[1]] = owner[...]
    table_ref[2:3, 0 : int_label.shape[1]] = int_label[...]


def pack_lists(task_amp, task_int, task_res, task_count, amp_label, owner, int_label):
    args = [task_amp, task_int, task_res, amp_label[None, :], owner, int_label[None, :]]
    return pl.pallas_call(
        lists_kernel,
        out_shape=[
            pltpu.VMEM((3,) + task_amp.shape, jnp.int32),
            pltpu.VMEM((3, DEEP), jnp.int32),
        ],
        in_specs=[pl.BlockSpec(memory_space=pltpu.SMEM)] + [HBM] * 6,
        out_specs=[VMEM] * 2,
        scratch_shapes=[pltpu.VMEM(x.shape, x.dtype) for x in args]
        + [pltpu.SemaphoreType.DMA((6,))],
        compiler_params=limit(0),
        cost_estimate=cost(0, 4096),
        name="pack_lists",
    )(task_count, *[in_hbm(x) for x in args])


def load_kernel(first, amp_hbm, out_ref, rows_ref, sems):
    amp_dev = amp_hbm.shape[0]
    rows = rows_ref.shape[0]
    copies = [
        pltpu.make_async_copy(amp_hbm.at[:, first + i, :], rows_ref.at[i], sems.at[i])
        for i in range(rows)
    ]
    for copy in copies:
        copy.start()
    for i, copy in enumerate(copies):
        copy.wait()
        hi, lo = split(rows_ref[i])
        at = 2 * amp_dev * i
        out_ref[at : at + amp_dev, :] = hi
        out_ref[at + amp_dev : at + 2 * amp_dev, :] = lo


def load(amplitudes, first, rows):
    amp_dev, _, depth = amplitudes.shape
    return pl.pallas_call(
        functools.partial(load_kernel, first),
        out_shape=pltpu.VMEM((rows * 2 * amp_dev, depth), jnp.bfloat16),
        in_specs=[HBM],
        out_specs=VMEM,
        scratch_shapes=[
            pltpu.VMEM((rows, amp_dev, depth), jnp.float32),
            pltpu.SemaphoreType.DMA((rows,)),
        ],
        compiler_params=limit(8 * rows * amp_dev * depth),
        cost_estimate=cost(0, 8 * rows * amp_dev * depth),
        name="load_amplitudes",
    )(in_hbm(amplitudes))


def coefficients(lists_ref, table_ref, amp_dev, lanes, blocks):
    lane = lax.axis_index("wide")
    grp = lax.axis_index("grp")
    amp, cint, res = (lists_ref[i] for i in range(3))
    local = amp - lane * amp_dev
    valid = (res >= 0) & (local >= 0) & (local < amp_dev)
    pos = jnp.zeros_like(res)
    for p in range(lanes):
        pos = jnp.where(res == table_ref[1:2, p : p + 1], p, pos)
    offset = pos ^ lane
    place = jnp.zeros_like(res)
    away, side = tile_order(lanes)
    for j, k in enumerate(away + side):
        place = jnp.where(offset == k, j, place)
    seg = jnp.where(valid, place * blocks + (cint ^ grp), -1)
    half = lanes // 2
    group = DEEP // (2 * amp_dev)
    rows = 2 * blocks * group * half
    slots = amp.shape[1]

    def parts(row):
        tile = row & (half - 1)
        inner = (row >> (half.bit_length() - 1)) & (group - 1)
        outer = row >> ((half * group).bit_length() - 1)
        return tile, inner, outer & (blocks - 1), outer >> (blocks.bit_length() - 1)

    tile, _, block, away_or_side = parts(lax.broadcasted_iota(jnp.int32, (rows, slots), 0))
    row_seg = (away_or_side * half + tile) * blocks + block
    col_amp = lax.broadcasted_iota(jnp.int32, (DEEP, slots), 0) & (amp_dev - 1)
    counts = jnp.zeros((rows, DEEP), jnp.float32)
    for src in range(lanes):
        hit_row = jnp.where(row_seg == seg[src : src + 1, :], 1.0, 0.0)
        hit_col = jnp.where(col_amp == local[src : src + 1, :], 1.0, 0.0)
        counts += lax.dot_general(
            hit_row.astype(jnp.bfloat16),
            hit_col.astype(jnp.bfloat16),
            (((1,), (1,)), ((), ())),
            preferred_element_type=jnp.float32,
        )
    _, inner, block, _ = parts(lax.broadcasted_iota(jnp.int32, (rows, DEEP), 0))
    block = block ^ grp
    label = jnp.zeros((rows, DEEP), jnp.int32)
    for c in range(blocks):
        label = jnp.where(block == c, table_ref[2:3, c : c + 1], label)
    odd = (label + table_ref[0:1, :]) & 1
    col = lax.broadcasted_iota(jnp.int32, (rows, DEEP), 1)
    same = inner == (col >> ((2 * amp_dev).bit_length() - 1))
    weight = jnp.where(odd == 1, -counts, counts)
    return jnp.where(same, weight, 0.0).astype(jnp.bfloat16)


def passes(hi, lo, in_hi, in_lo):
    dot = functools.partial(jnp.dot, preferred_element_type=jnp.float32)
    return dot(hi, in_hi) + dot(hi, in_lo) + dot(lo, in_hi)


def store_tiles(out, out_refs, held):
    tiles = len(out_refs)
    rows = out.shape[0] // tiles
    for b in range(held.shape[0]):
        held[b] = out[:, b * LANES : (b + 1) * LANES]
    for j, ref in enumerate(out_refs):
        for b in range(held.shape[0]):
            ref[0, :, b * LANES : (b + 1) * LANES] = held[b, pl.ds(j, rows, stride=tiles), :]


def sums_kernel(lanes, blocks, amp_dev, lists_ref, table_ref, own_ref, pair_ref, *refs):
    amp_refs, sums_refs, (local_ref, in_hi, in_lo) = refs[:2], refs[2:6], refs[6:]
    weight = coefficients(lists_ref, table_ref, amp_dev, lanes, blocks)
    depth = own_ref.shape[0]
    step = weight.shape[0] // (2 * blocks)
    first = 0
    for ref in amp_refs:
        count = ref.shape[0] // DEEP
        for g in range(count):
            rows = ref[g * DEEP : (g + 1) * DEEP, :]
            total = jnp.dot(weight, rows, preferred_element_type=jnp.float32)
            at = slice((first + g) * step, (first + g + 1) * step)
            for k in range(2):
                for c in range(blocks):
                    r = (k * blocks + c) * step
                    hi, lo = split(total[r : r + step, :])
                    sums_refs[2 * k][at, c * depth : (c + 1) * depth] = hi
                    sums_refs[2 * k + 1][at, c * depth : (c + 1) * depth] = lo
        first += count
    for c, ref in enumerate((own_ref, pair_ref)):
        hi, lo = split(ref[...])
        in_hi[c * depth : (c + 1) * depth, :] = hi
        in_lo[c * depth : (c + 1) * depth, :] = lo
    hi, lo = (x[:, : 2 * depth] for x in sums_refs[:2])
    local_ref[...] = passes(hi, lo, in_hi[...], in_lo[...])


def sums(lists, table, own, pair, rows, amp_dev, tile_rows, lanes, blocks):
    depth, window = own.shape
    kept = lanes // 2 * tile_rows
    held = pltpu.VMEM((kept, blocks * depth), jnp.bfloat16)
    local = pltpu.VMEM((2 * depth, window), jnp.bfloat16)
    product = pltpu.VMEM((kept, window), jnp.float32)
    return pl.pallas_call(
        functools.partial(sums_kernel, lanes, blocks, amp_dev),
        out_shape=[held] * 4 + [product] + [local] * 2,
        in_specs=[VMEM] * (4 + len(rows)),
        out_specs=[VMEM] * 7,
        compiler_params=limit(16 * depth * window),
        cost_estimate=cost(0, 16 * tile_rows * amp_dev * depth),
        name="sums",
    )(lists, table, own, pair, *[in_vmem(x) for x in rows])


def split_parts(parts, in_hi, in_lo):
    depth = sum(x.shape[0] for x in parts[:3])
    mine, theirs = end_offsets(depth)
    for c in range(len(parts) // 3):
        starts = (mine, row_cuts(depth)[0], theirs)
        for start, part in zip(starts, parts[3 * c : 3 * c + 3]):
            hi, lo = split(part[...])
            at = pl.ds(pl.multiple_of(c * depth + start, 16), part.shape[0])
            in_hi[at, :] = hi
            in_lo[at, :] = lo


def columns(x, odd, depth):
    blocks = range(2 + odd, x.shape[1] // depth, 2)
    return jnp.concatenate([x[:, c * depth : (c + 1) * depth] for c in blocks], axis=1)


def fetched_kernel(*refs):
    sums_refs, (local_ref, local_hi, local_lo), rest = refs[:4], refs[4:7], refs[7:]
    parts, out_refs, (in_hi, in_lo) = rest[:-4], rest[-4:-2], rest[-2:]
    depth = sum(x.shape[0] for x in parts[:3])
    split_parts(parts, in_hi, in_lo)
    hi, lo = (x[:, : 2 * depth] for x in sums_refs[2:])
    out_refs[1][...] = passes(hi, lo, local_hi[...], local_lo[...])
    for k, ref in enumerate((local_ref, out_refs[1])):
        hi, lo = (columns(x, 0, depth) for x in sums_refs[2 * k : 2 * k + 2])
        out_refs[k][...] = ref[...] + passes(hi, lo, in_hi[...], in_lo[...])


def flat(parts):
    return [x for three in parts for x in three]


def fetched_products(held, local, parts):
    rows, window = local[0].shape
    depth = sum(x.shape[0] for x in parts[0])
    half = pltpu.VMEM((len(parts) * depth, window), jnp.bfloat16)
    return pl.pallas_call(
        fetched_kernel,
        out_shape=[pltpu.VMEM((rows, window), jnp.float32)] * 2,
        in_specs=[VMEM] * (7 + 3 * len(parts)),
        out_specs=[VMEM] * 2,
        scratch_shapes=[half] * 2,
        compiler_params=limit(16 * len(parts) * depth * window),
        cost_estimate=cost(12 * rows * len(parts) * depth * window, 0),
        name="fetched_products",
    )(*[in_vmem(x) for x in (*held, *local)], *flat(parts))


def away_kernel(tiles, hi, lo, local_ref, *rest):
    parts, out_refs, (in_hi, in_lo, held) = rest[: -3 - tiles], rest[-3 - tiles : -3], rest[-3:]
    split_parts(parts, in_hi, in_lo)
    depth = sum(x.shape[0] for x in parts[:3])
    out = passes(columns(hi, 1, depth), columns(lo, 1, depth), in_hi[...], in_lo[...])
    store_tiles(local_ref[...] + out, out_refs, held)


def side_kernel(depth, hi, lo, local_ref, in_hi, in_lo, *rest):
    out_refs, held = rest[:-1], rest[-1]
    out = passes(columns(hi, 1, depth), columns(lo, 1, depth), in_hi[...], in_lo[...])
    store_tiles(local_ref[...] + out, out_refs, held)


def away_products(hi, lo, local, parts, tiles):
    rows, window = local.shape
    depth = sum(x.shape[0] for x in parts[0])
    remote = pltpu.VMEM((len(parts) * depth, window), jnp.bfloat16)
    shapes = [jax.ShapeDtypeStruct((1, rows // tiles, window), jnp.float32)] * tiles
    *out, in_hi, in_lo = pl.pallas_call(
        functools.partial(away_kernel, tiles),
        out_shape=shapes + [remote] * 2,
        in_specs=[VMEM] * (3 + 3 * len(parts)),
        out_specs=[VMEM] * (tiles + 2),
        scratch_shapes=[pltpu.VMEM((window // LANES, rows, LANES), jnp.float32)],
        compiler_params=limit(16 * len(parts) * depth * window),
        cost_estimate=cost(6 * rows * len(parts) * depth * window, 0),
        name="away_products",
    )(*[in_vmem(x) for x in (hi, lo, local)], *flat(parts))
    return out, in_hi, in_lo


def side_products(hi, lo, local, in_hi, in_lo, tiles, depth):
    rows, window = local.shape
    shapes = [jax.ShapeDtypeStruct((1, rows // tiles, window), jnp.float32)] * tiles
    return pl.pallas_call(
        functools.partial(side_kernel, depth),
        out_shape=shapes,
        in_specs=[VMEM] * 5,
        out_specs=[VMEM] * tiles,
        scratch_shapes=[pltpu.VMEM((window // LANES, rows, LANES), jnp.float32)],
        compiler_params=limit(0),
        cost_estimate=cost(0, 0),
        name="side_products",
    )(*[in_vmem(x) for x in (hi, lo, local, in_hi, in_lo)])


def on_device(
    amplitudes,
    integrals,
    base_residual,
    occ_gap,
    virt_sum,
    task_amp,
    task_int,
    task_res,
    task_count,
    res_owner,
    amp_label,
    int_label,
):
    lanes = lax.axis_size("wide")
    grps = lax.axis_size("grp")
    amp_dev, tile_rows, _ = amplitudes.shape
    half = lanes // 2
    own = integrals[0]
    one, two = piece(own, True), piece(own, False)
    fetched = {k: [swap(x, "grp", k) for x in (one, two)] for k in range(2, grps, 2)}
    lists, table = pack_lists(
        task_amp, task_int, after(task_res, one), task_count, amp_label, res_owner, int_label
    )
    pair = swap(own, "grp", 1)
    rows = [load(amplitudes, i * tile_rows // 2, tile_rows // 2) for i in range(2)]
    order = [1] + [1 << b for b in range(lanes.bit_length() - 2, 0, -1)]
    for k in order:
        if k == order[1]:
            lists = after(lists, rows[0])
        lists = jnp.concatenate([lists, swap(lists, "wide", k)], axis=1)
    lists = after(lists, rows[1])
    *held, local_away, local_hi, local_lo = sums(
        lists, table, own, pair, rows, amp_dev, tile_rows, lanes, grps
    )

    even, odd = [], []
    for k, (one, two) in fetched.items():
        even.append([one, two, swap(one, "wide", 1)])
        odd.append([swap(after(x, y), "grp", 1) for x, y in zip(even[-1], (lists, held[0], held[0]))])

    local = fetched_products(held, (local_away, local_hi, local_lo), even)
    away, in_hi, in_lo = away_products(*held[:2], local[0], odd, half)
    _, offsets = tile_order(lanes)
    far, near, last = range(lanes // 4), range(lanes // 4, half - 1), half - 1
    side = side_products(*held[2:], local[1], in_hi, in_lo, half, own.shape[0])
    got = [swap(after(away[j], side[0]) if j else away[j], "wide", 1) for j in far]
    summed = base_residual + side[last]
    for j in far:
        summed = summed + swap(side[j] + got[j], "wide", offsets[j])
    rest = away[last]
    for j in near:
        summed = summed + swap(side[j], "wide", offsets[j])
        rest = rest + swap(away[j], "wide", offsets[j])
    summed = summed + swap(rest, "wide", 1)
    divisor = occ_gap[:, :, None] + virt_sum[None, None, :]
    return summed / divisor


def solution(mesh):
    return jax.shard_map(
        on_device,
        mesh=mesh,
        in_specs=(
            P(("grp", "wide"), None, None),
            P("grp", None, None),
            P(("grp", "wide"), None, None),
            P(("grp", "wide"), None),
            P(),
            P(("grp", "wide"), None),
            P(("grp", "wide"), None),
            P(("grp", "wide"), None),
            P(("grp", "wide")),
            P("grp", None),
            P(("grp", "wide")),
            P(),
        ),
        out_specs=P(("grp", "wide"), None, None),
        check_vma=False,
    )
```
